256 devices in a mesh: blk: 8 (over y_lo, x), rows: 32 (over y_hi, z, core).
Axes of the slice: x: 4, y: 4 (y_hi: 2, y_lo: 2; y = y_hi * 2 + y_lo), z: 8, core: 2. Of those that a mesh axis runs over, the one named last changes fastest.
Arguments:
- embeddings: bfloat16 [524288, 768], P(('blk', 'rows')), may hold values from -6 to 6
- coverage: float32 [524288], P(('blk', 'rows')), may hold values from 0 to 4
- chosen_index: int32 [512], replicated, may hold values from 0 to 524287, as said below
- candidate_index: int32 [1024], P('blk'), may hold values from 0 to 524287, as said below
Outputs:
- new_coverage: float32 [524288], P(('blk', 'rows'))
- gains: float32 [1024], P(('blk', 'rows'))
The draws below stay inside these ranges and needn't reach their ends.
Inputs may be any that keep to these rules, and one draw needn't show every extreme that they name: `chosen_index`: the entries are distinct; the rows r * 2048 to (r + 1) * 2048 - 1 hold at most 4 of them for every r, and exactly 4 for some r. `candidate_index`: entries b * 128 to (b + 1) * 128 - 1 lie in rows b * 65536 to (b + 1) * 65536 - 1.
All inputs are finite; a program needn't handle non-finite values.
Results may differ from the reference program's by a relative error of at most 0.00035.
Values may be sent and summed in bfloat16 or wider, within the bound.
No kernel may reach another device: no remote copies, remote signals or barrier semaphores. Data moves between devices by JAX's collectives and lax.ppermute only.
A program may use at most 64 MiB of HBM per device.

```python
import jax
import jax.numpy as jnp
from jax import lax

D = 768
ROWS_DEV = 2048
CAND_BLOCK = 128
MOST = 4
N = 524288
GROUP = 65536
CHOSEN = 512
N_BLK = 8
DEVICES = 256


def draw_chosen_index(key, part):
    key_count = jax.random.fold_in(key, 11)
    key_spot = jax.random.fold_in(key, 12)
    key_perm = jax.random.fold_in(key, 13)
    key_shuffle = jax.random.fold_in(key, 14)
    halves = DEVICES // 2
    counts_half = jax.random.randint(key_count, (halves,), 0, MOST + 1)
    spot = jax.random.randint(key_spot, (), 0, halves)
    counts_half = counts_half.at[spot].set(MOST)
    counts = jnp.stack([counts_half, MOST - counts_half], axis=1).reshape(DEVICES)
    device_keys = jax.random.split(key_perm, DEVICES)
    perms = jax.vmap(lambda kk: jax.random.permutation(kk, ROWS_DEV))(device_keys)
    picked_local = perms[:, :MOST].astype(jnp.int32)
    offsets = (jnp.arange(DEVICES, dtype=jnp.int32) * ROWS_DEV)[:, None]
    globals_rows = (picked_local + offsets).reshape(DEVICES * MOST)
    valid = (jnp.arange(MOST, dtype=jnp.int32)[None, :] < counts[:, None]).reshape(DEVICES * MOST)
    order = jnp.argsort(jnp.where(valid, 0, 1).astype(jnp.int32), stable=True)[:CHOSEN]
    selected = globals_rows[order]
    return jax.random.permutation(key_shuffle, selected).astype(jnp.int32)


def draw_candidate_index(key, part):
    key_rows = jax.random.fold_in(key, 21)
    inside = jax.random.randint(key_rows, (N_BLK, CAND_BLOCK), 0, GROUP)
    offsets = (jnp.arange(N_BLK, dtype=jnp.int32) * GROUP)[:, None]
    return (inside + offsets).reshape(N_BLK * CAND_BLOCK).astype(jnp.int32)


def steps_of(rng, dims, shards, least, largest):
    level, own = 1.0, jax.random.fold_in(rng, 6)
    for dim, parts in shards:
        draws = jnp.exp(jax.random.uniform(jax.random.fold_in(own, dim), (parts,), jnp.float32, least / len(shards), largest / len(shards)))
        level = level * jnp.repeat(draws, dims[dim] // parts).reshape([-1 if axis == dim else 1 for axis in range(len(dims))])
    return level


def normal_values(own_key, extent, scale, reach, cuts=(), kind=jnp.bfloat16):
    result = jax.random.normal(own_key, extent, jnp.float32) * scale
    if len(cuts) > 0:
        result = steps_of(own_key, extent, cuts, -0.22, 0.18) * result
    return jnp.clip(result, min=-reach, max=reach).astype(kind)


def setup_inputs(seed: int = 0) -> dict:
    arg_keys = jax.random.split(jax.random.key(seed), 5)
    embeddings = normal_values(arg_keys[0], (N, D), 1.0, 6.0, ((0, 256),))
    coverage = jnp.clip(4.0 * jax.random.uniform(arg_keys[1], (N,), jnp.float32) ** steps_of(arg_keys[1], (N,), ((0, 256),), -0.2, 0.2), 0.0, 4.0)
    chosen_index = draw_chosen_index(jax.random.fold_in(arg_keys[4], 71), 0)
    candidate_index = draw_candidate_index(jax.random.fold_in(arg_keys[4], 71), 0)
    return dict(embeddings=embeddings, coverage=coverage, chosen_index=chosen_index, candidate_index=candidate_index)


def reference(embeddings, coverage, chosen_index, candidate_index):
    scale = 1.0 / (D ** 0.5)
    chosen = embeddings[chosen_index].astype(jnp.float32)
    candidates = embeddings[candidate_index].astype(jnp.float32)
    blocks = embeddings.reshape(N // ROWS_DEV, ROWS_DEV, D)
    covers = coverage.reshape(N // ROWS_DEV, ROWS_DEV)

    def one_block(pair):
        rows_block, cover_block = pair
        rows_block = rows_block.astype(jnp.float32)
        sims = jnp.dot(rows_block, chosen.T, preferred_element_type=jnp.float32) * scale
        updated = jnp.maximum(cover_block, jnp.max(sims, axis=1))
        cand_sims = jnp.dot(rows_block, candidates.T, preferred_element_type=jnp.float32) * scale
        partial_gain = jnp.sum(jnp.maximum(cand_sims - updated[:, None], 0.0), axis=0)
        return updated, partial_gain

    updated, partial_gain = lax.map(one_block, (blocks, covers))
    return updated.reshape(N), jnp.sum(partial_gain, axis=0)
```

```python
import jax
import jax.numpy as jnp
from jax import lax
from jax.sharding import Mesh
from jax.sharding import PartitionSpec as P

AXES = ("ylo", "x", "yhi", "z", "core")
BLK = ("ylo", "x")
YHI_Z = ("yhi", "z")
YX = ("ylo", "x", "yhi")
MOST = 4
SWAP = [(0, 1), (1, 0)]


def local(embeddings, coverage, chosen_index, candidate_index):
    rows, width = embeddings.shape
    scale = 1.0 / width**0.5
    core = lax.axis_index("core")
    yhi = lax.axis_index("yhi")
    base = lax.axis_index(AXES) * rows

    off = chosen_index - base
    inside = (off >= 0) & (off < rows)
    rank = jnp.sum(inside[None, :] & (off[None, :] < off[:, None]), axis=1)
    slot = inside[None, :] & (rank[None, :] == jnp.arange(MOST)[:, None])
    spots = jnp.max(jnp.where(slot, off[None, :], -1), axis=1)
    targets = jnp.concatenate([candidate_index - base, spots, jnp.full((MOST,), -1, jnp.int32)])
    pick = (targets[:, None] == jnp.arange(rows)[None, :]).astype(jnp.bfloat16)
    picked = jnp.dot(pick, embeddings, preferred_element_type=jnp.float32).astype(jnp.bfloat16)

    cands = picked[:128].reshape(2, 2, 32, width)
    chosen = picked[128 : 128 + MOST]
    mine = lax.dynamic_index_in_dim(cands, core, 1, keepdims=False)
    theirs = lax.dynamic_index_in_dim(cands, 1 - core, 1, keepdims=False)
    half = mine + lax.ppermute(theirs, "core", SWAP)

    send = jnp.concatenate(
        [
            jnp.broadcast_to(half[:, None], (2, 8, 32, width)),
            jnp.broadcast_to(chosen, (2, 8, MOST, width)),
        ],
        axis=2,
    ).reshape(16, 32 + MOST, width)
    got = lax.all_to_all(send, YHI_Z, 0, 0)
    quarter = jnp.sum(got[:, :32].astype(jnp.float32), axis=0).astype(jnp.bfloat16)
    near = lax.dynamic_slice_in_dim(got[:, 32:], yhi * 8, 8, 0).reshape(8 * MOST, width)

    block = jnp.concatenate([quarter, near], axis=0)
    all_xy = lax.all_to_all(jnp.broadcast_to(block, (16, 64, width)), YX, 0, 0)
    other = lax.ppermute(all_xy, "core", SWAP)
    first = jnp.where(core == 0, all_xy, other)
    second = jnp.where(core == 0, other, all_xy)
    both = jnp.stack([first, second], axis=1)

    all_chosen = both[:, :, 32:].reshape(1024, width)
    all_cands = both[:, :, :32].reshape(1024, width)
    sims = jnp.dot(embeddings, all_chosen.T, preferred_element_type=jnp.float32) * scale
    new_coverage = jnp.maximum(coverage, jnp.max(sims, axis=1))
    cand_sims = jnp.dot(embeddings, all_cands.T, preferred_element_type=jnp.float32) * scale
    part = jnp.sum(jnp.maximum(cand_sims - new_coverage[:, None], 0.0), axis=0)
    parts = lax.all_to_all(part.reshape(256, 4), AXES, 0, 0)
    gains = jnp.sum(parts, axis=0)
    return new_coverage, gains


def solution(mesh):
    torus = Mesh(mesh.devices.reshape(2, 4, 2, 8, 2), AXES)
    return jax.shard_map(
        local,
        mesh=torus,
        in_specs=(P(AXES, None), P(AXES), P(), P(BLK)),
        out_specs=(P(AXES), P(AXES)),
        check_vma=False,
    )
```

```python
import jax
import jax.numpy as jnp
from jax import lax
from jax.sharding import Mesh
from jax.sharding import PartitionSpec as P

AXES = ("ylo", "x", "yhi", "z", "core")
SIZES = (2, 4, 2, 8, 2)
BLK = ("ylo", "x")
CHIPS = ("ylo", "x", "yhi", "z")
MOST = 4


def place(y, x, z, core):
    return (((y % 2) * 4 + x) * 2 + y // 2) * 16 + z * 2 + core


def pairs_of(move):
    return [
        (place(y, x, z, core), place(*move(y, x, z, core)))
        for y in range(4)
        for x in range(4)
        for z in range(8)
        for core in range(2)
    ]


def swap(value, y_mask, core_mask):
    return lax.ppermute(value, AXES, pairs_of(lambda y, x, z, c: (y ^ y_mask, x, z, c ^ core_mask)))


def turn(value, mask, first):
    return lax.ppermute(
        value,
        AXES,
        pairs_of(lambda y, x, z, c: (y, x ^ mask, z, c) if (c == 0) == first else (y ^ mask, x, z, c)),
    )


def flipped(flag, value, dim):
    return jnp.where(flag == 1, jnp.flip(value, dim), value)


def local(embeddings, coverage, chosen_index, candidate_index):
    rows, width = embeddings.shape
    scale = 1.0 / width**0.5
    core = lax.axis_index("core")
    yhi = lax.axis_index("yhi")
    ylo = lax.axis_index("ylo")
    x = lax.axis_index("x")
    base = lax.axis_index(AXES) * rows

    partner = swap(embeddings, 0, 1)

    off = chosen_index - base
    inside = (off >= 0) & (off < rows)
    rank = jnp.sum(inside[None, :] & (off[None, :] < off[:, None]), axis=1)
    slot = inside[None, :] & (rank[None, :] == jnp.arange(MOST)[:, None])
    spots = jnp.max(jnp.where(slot, off[None, :], -1), axis=1)
    wanted = (candidate_index - base).reshape(2, 8, 2, 4).transpose(0, 2, 1, 3)
    wanted = flipped(yhi, flipped(core, wanted, 1), 0).reshape(128)
    targets = jnp.concatenate([wanted, spots, jnp.full((MOST,), -1, jnp.int32)])
    pick = (targets[:, None] == jnp.arange(rows)[None, :]).astype(jnp.bfloat16)
    picked = jnp.dot(pick, embeddings, preferred_element_type=jnp.float32).astype(jnp.bfloat16)

    quarter = (
        picked[:32]
        + swap(picked[32:64], 0, 1)
        + swap(picked[64:96], 2, 0)
        + swap(picked[96:128], 2, 1)
    )
    send = jnp.concatenate([quarter, picked[128 : 128 + MOST]], axis=0)
    got = lax.all_to_all(jnp.broadcast_to(send, (8, 32 + MOST, width)), "z", 0, 0)
    quarter = jnp.sum(got[:, :32].astype(jnp.float32), axis=0).astype(jnp.bfloat16)
    near = got[:, 32:].reshape(8 * MOST, width)

    block = jnp.concatenate([quarter, near], axis=0)
    line = jnp.stack([block] + [turn(block, s, True) for s in (1, 2, 3)])
    plane = [line] + [turn(line, s, False) for s in (1, 2, 3)]
    cands = jnp.concatenate([p[:, :32] for p in plane]).reshape(512, width)
    chosen = jnp.concatenate([p[:, 32:] for p in plane]).reshape(512, width)

    def best(table):
        return jnp.max(jnp.dot(table, chosen.T, preferred_element_type=jnp.float32) * scale, axis=1)

    best_own = jnp.maximum(coverage, best(embeddings))
    best_partner = best(partner)
    swapped = swap(jnp.stack([best_own, best_partner]), 0, 1)
    new_coverage = jnp.maximum(best_own, swapped[1])
    cover_partner = jnp.maximum(best_partner, swapped[0])

    def gain(table, cover):
        sims = jnp.dot(table, cands.T, preferred_element_type=jnp.float32) * scale
        return jnp.sum(jnp.maximum(sims - cover[:, None], 0.0), axis=0)

    part = gain(embeddings, new_coverage) + gain(partner, cover_partner)
    part = part.reshape(4, 4, 32)
    part = jnp.where(core == 0, part, part.transpose(1, 0, 2)).reshape(2, 2, 2, 2, 32)
    part = flipped(ylo, flipped(yhi, part, 0), 1)
    part = flipped(x % 2, flipped(x // 2, part, 2), 3)
    part = part.transpose(1, 2, 3, 0, 4).reshape(128, 4)
    parts = lax.all_to_all(part, CHIPS, 0, 0)
    return new_coverage, jnp.sum(parts, axis=0)


def solution(mesh):
    torus = Mesh(mesh.devices.reshape(SIZES), AXES)
    return jax.shard_map(
        local,
        mesh=torus,
        in_specs=(P(AXES, None), P(AXES), P(), P(BLK)),
        out_specs=(P(AXES), P(AXES)),
        check_vma=False,
    )
```

```python
import functools

import jax
import jax.numpy as jnp
from jax import lax
from jax.experimental import pallas as pl
from jax.experimental.pallas import tpu as pltpu
from jax.sharding import Mesh
from jax.sharding import PartitionSpec as P

AXES = ("ylo", "x", "yhi", "z", "core")
SIZES = (2, 4, 2, 8, 2)
BLK = ("ylo", "x")
CHIPS = ("ylo", "x", "yhi", "z")
MOST = 4
STEP = 512


def place(y, x, z, core):
    return (((y % 2) * 4 + x) * 2 + y // 2) * 16 + z * 2 + core


def pairs_of(move):
    return [
        (place(y, x, z, core), place(*move(y, x, z, core)))
        for y in range(4)
        for x in range(4)
        for z in range(8)
        for core in range(2)
    ]


def swap(value, y_mask, core_mask):
    return lax.ppermute(value, AXES, pairs_of(lambda y, x, z, c: (y ^ y_mask, x, z, c ^ core_mask)))


def turn(value, mask, first):
    return lax.ppermute(
        value,
        AXES,
        pairs_of(lambda y, x, z, c: (y, x ^ mask, z, c) if (c == 0) == first else (y ^ mask, x, z, c)),
    )


def turned_table(pieces, turned):
    for k, piece in enumerate(pieces):
        turned[:, k * 128 : k * 128 + 128] = piece[...].T


def tile_sims(table, turned, start):
    return jnp.dot(table[pl.ds(start, STEP), :], turned[...], preferred_element_type=jnp.float32)


def fetches(source, target, arrivals):
    step = target.shape[0] // arrivals.shape[0]
    parts = [pl.ds(k * step, step) for k in range(arrivals.shape[0])]
    return [
        pltpu.make_async_copy(source.at[at, :], target.at[at, :], arrivals.at[k])
        for k, at in enumerate(parts)
    ]


def best_kernel(own_ref, coverage_ref, c0, c1, c2, c3, partner_ref, best_ref, partner, turned, arrivals):
    rows, width = own_ref.shape
    scale = 1.0 / width**0.5
    copies = fetches(partner_ref, partner, arrivals)
    for copy in copies:
        copy.start()
    turned_table((c0, c1, c2, c3), turned)
    for t, table in enumerate((own_ref, partner)):
        for k, start in enumerate(range(0, rows, STEP)):
            if t == 1:
                copies[k].wait()
            sims = tile_sims(table, turned, start)
            top = functools.reduce(jnp.maximum, [sims[:, l : l + 128] for l in range(0, 512, 128)])
            for r in range(0, STEP, 128):
                here = pl.ds(start + r, 128)
                row = jnp.max(top[r : r + 128].T, axis=0, keepdims=True) * scale
                if t == 0:
                    row = jnp.maximum(row, coverage_ref[:, here])
                best_ref[t : t + 1, here] = row


def gain_kernel(own_ref, cover_ref, c0, c1, c2, c3, partner_ref, gain_ref, partner, turned, arrivals):
    rows, width = own_ref.shape
    scale = 1.0 / width**0.5
    copies = fetches(partner_ref, partner, arrivals)
    for copy in copies:
        copy.start()
    turned_table((c0, c1, c2, c3), turned)
    total = jnp.zeros((8, 512), jnp.float32)
    for t, table in enumerate((own_ref, partner)):
        for k, start in enumerate(range(0, rows, STEP)):
            if t == 1:
                copies[k].wait()
            sims = tile_sims(table, turned, start)
            for r in range(0, STEP, 128):
                line = cover_ref[t : t + 1, pl.ds(start + r, 128)] * width**0.5
                floor = jnp.broadcast_to(line, (128, 128)).T
                over = jnp.maximum(sims[r : r + 128] - jnp.concatenate([floor] * 4, axis=1), 0.0)
                total = total + jnp.sum(over.reshape(16, 8, 512), axis=0)
    sums = jnp.sum(total, axis=0, keepdims=True) * scale
    first = lax.axis_index("core") == 0
    x = lax.axis_index("x")
    yhi, ylo = lax.axis_index("yhi"), lax.axis_index("ylo")
    for late in range(4):
        for early in range(4):
            x_mask = jnp.where(first, early, late)
            y_mask = jnp.where(first, late, early)
            at = ((ylo ^ (y_mask & 1)) * 4 + (x ^ x_mask)) * 2 + (yhi ^ (y_mask >> 1))
            lane = late * 128 + early * 32
            gain_ref[pl.ds(at, 1), :] = sums[:, lane : lane + 32]


def on_chip(kernel, out, *operands):
    rows, width = operands[0].shape
    vmem = pl.BlockSpec(memory_space=pltpu.VMEM)
    return pl.pallas_call(
        kernel,
        out_shape=jax.ShapeDtypeStruct(out, jnp.float32),
        in_specs=[vmem] * (len(operands) - 1) + [pl.BlockSpec(memory_space=pl.ANY)],
        out_specs=vmem,
        scratch_shapes=[
            pltpu.VMEM((rows, width), jnp.bfloat16),
            pltpu.VMEM((width, 512), jnp.bfloat16),
            pltpu.SemaphoreType.DMA((rows // STEP,)),
        ],
        compiler_params=pltpu.CompilerParams(vmem_limit_bytes=24 << 20),
        cost_estimate=pl.CostEstimate(flops=4096 * 512 * 768 * 2, bytes_accessed=8 << 20, transcendentals=0),
    )(*operands)


def pick_kernel(chosen_ref, cand_ref, table_ref, q0, q1, q2, q3, chosen_rows_ref, table, arrivals):
    rows, width = table.shape
    copies = fetches(table_ref, table, arrivals)
    for copy in copies:
        copy.start()
    core, yhi = lax.axis_index("core"), lax.axis_index("yhi")
    base = lax.axis_index(AXES) * rows

    lane = lax.broadcasted_iota(jnp.int32, (8, 128), 1)
    quarter = lane >> 5
    source = ((yhi ^ (quarter >> 1)) << 6) | ((lane & 28) << 1) | ((core ^ (quarter & 1)) << 2) | (lane & 3)
    wanted = jnp.take_along_axis(jnp.broadcast_to(cand_ref[...], (8, 128)), source, axis=1) - base
    wanted = jnp.broadcast_to(wanted[:1], (128, 128)).T

    left = chosen_ref[...] - base
    left = jnp.where((left >= 0) & (left < rows), left, rows).astype(jnp.float32)
    row = lax.broadcasted_iota(jnp.int32, (8, 128), 0)
    spots = jnp.full((8, 128), -1, jnp.int32)
    for s in range(MOST):
        least = jnp.min(jnp.min(left, axis=0, keepdims=True), axis=1, keepdims=True)
        left = jnp.where(left == least, float(rows), left)
        spots = jnp.where(row == s, least.astype(jnp.int32), spots)

    targets = jnp.concatenate([wanted, spots], axis=0)
    total = jnp.zeros((136, width), jnp.float32)
    step = rows // len(copies)
    lanes = lax.broadcasted_iota(jnp.int32, (136, 128), 1)
    for k, copy in enumerate(copies):
        hits = [targets == lanes + (k * step + l) for l in range(0, step, 128)]
        pick = jnp.concatenate([jnp.where(h, 1.0, 0.0) for h in hits], axis=1).astype(jnp.bfloat16)
        copy.wait()
        total = total + jnp.dot(pick, table[pl.ds(k * step, step), :], preferred_element_type=jnp.float32)
    picked = total.astype(jnp.bfloat16)
    for k, out in enumerate((q0, q1, q2, q3)):
        out[...] = picked[k * 32 : k * 32 + 32]
    chosen_rows_ref[...] = total[128 : 128 + MOST].astype(jnp.bfloat16)


def own_picks(chosen_index, candidate_index, embeddings):
    rows, width = embeddings.shape
    vmem = pl.BlockSpec(memory_space=pltpu.VMEM)
    return pl.pallas_call(
        pick_kernel,
        out_shape=[jax.ShapeDtypeStruct((32, width), jnp.bfloat16)] * 4
        + [jax.ShapeDtypeStruct((MOST, width), jnp.bfloat16)],
        in_specs=[vmem, vmem, pl.BlockSpec(memory_space=pl.ANY)],
        out_specs=[vmem] * 5,
        scratch_shapes=[pltpu.VMEM((rows, width), jnp.bfloat16), pltpu.SemaphoreType.DMA((8,))],
        compiler_params=pltpu.CompilerParams(vmem_limit_bytes=60 << 20),
        cost_estimate=pl.CostEstimate(flops=136 * 2048 * 768 * 2, bytes_accessed=4 << 20, transcendentals=0),
    )(chosen_index.reshape(4, 128), candidate_index.reshape(1, 128), embeddings)


def local(embeddings, coverage, chosen_index, candidate_index):
    rows, width = embeddings.shape
    q0, q1, q2, q3, found = own_picks(chosen_index, candidate_index, embeddings)
    q1, q2, q3, later = lax.optimization_barrier((q1, q2, q3, embeddings))
    partner = swap(later, 0, 1)
    quarter = q0 + swap(q1, 0, 1) + swap(q2, 2, 0) + swap(q3, 2, 1)
    send = jnp.concatenate([quarter, found], axis=0)
    got = lax.all_to_all(jnp.broadcast_to(send, (8, 32 + MOST, width)), "z", 0, 0)
    quarter = jnp.sum(got[:, :32].astype(jnp.float32), axis=0).astype(jnp.bfloat16)
    near = got[:, 32:].reshape(8 * MOST, width)

    block = jnp.concatenate([quarter, near], axis=0)
    line = jnp.stack([block] + [turn(block, s, True) for s in (1, 2, 3)])
    cands, chosen = line[:, :32].reshape(128, width), line[:, 32:].reshape(128, width)
    chosen = [chosen] + [turn(chosen, s, False) for s in (1, 2, 3)]
    cands = [cands] + [turn(cands, s, False) for s in (1, 2, 3)]

    best = on_chip(best_kernel, (2, rows), embeddings, coverage.reshape(1, rows), *chosen, partner)
    cover = jnp.maximum(best, swap(best, 0, 1)[::-1])
    part = on_chip(gain_kernel, (16, 32), embeddings, cover, *cands, partner).reshape(128, 4)
    parts = lax.all_to_all(part, CHIPS, 0, 0)
    return cover[0], jnp.sum(parts, axis=0)


def solution(mesh):
    torus = Mesh(mesh.devices.reshape(SIZES), AXES)
    return jax.shard_map(
        local,
        mesh=torus,
        in_specs=(P(AXES, None), P(AXES), P(), P(BLK)),
        out_specs=(P(AXES), P(AXES)),
        check_vma=False,
    )
```

```python
import functools

import jax
import jax.numpy as jnp
from jax import lax
from jax.experimental import pallas as pl
from jax.experimental.pallas import tpu as pltpu
from jax.sharding import Mesh
from jax.sharding import PartitionSpec as P

AXES = ("ylo", "x", "yhi", "z", "core")
SIZES = (2, 4, 2, 8, 2)
BLK = ("ylo", "x")
CHIPS = ("ylo", "x", "yhi", "z")
MOST = 4
STEP = 256


def place(y, x, z, core):
    return (((y % 2) * 4 + x) * 2 + y // 2) * 16 + z * 2 + core


def pairs_of(move):
    return [
        (place(y, x, z, core), place(*move(y, x, z, core)))
        for y in range(4)
        for x in range(4)
        for z in range(8)
        for core in range(2)
    ]


def swap(value, y_mask, core_mask):
    return lax.ppermute(value, AXES, pairs_of(lambda y, x, z, c: (y ^ y_mask, x, z, c ^ core_mask)))


def turn(value, mask, first):
    return lax.ppermute(
        value,
        AXES,
        pairs_of(lambda y, x, z, c: (y, x ^ mask, z, c) if (c == 0) == first else (y ^ mask, x, z, c)),
    )


def turned_table(pieces, turned):
    for k, piece in enumerate(pieces):
        turned[:, k * 128 : k * 128 + 128] = piece[...].T


def tile_sims(table, turned, start):
    return jnp.dot(table[pl.ds(start, STEP), :], turned[...], preferred_element_type=jnp.float32)


def turn_kernel(c0, c1, c2, c3, turned):
    turned_table((c0, c1, c2, c3), turned)


def turned_pieces(pieces):
    vmem = pl.BlockSpec(memory_space=pltpu.VMEM)
    return pl.pallas_call(
        turn_kernel,
        out_shape=jax.ShapeDtypeStruct((pieces[0].shape[1], 512), jnp.bfloat16),
        in_specs=[vmem] * 4,
        out_specs=vmem,
        compiler_params=pltpu.CompilerParams(vmem_limit_bytes=8 << 20),
        cost_estimate=pl.CostEstimate(flops=1 << 20, bytes_accessed=2 << 20, transcendentals=0),
    )(*pieces)


def fetches(source, target, arrivals):
    step = target.shape[0] // arrivals.shape[0]
    parts = [pl.ds(k * step, step) for k in range(arrivals.shape[0])]
    return [
        pltpu.make_async_copy(source.at[at, :], target.at[at, :], arrivals.at[k])
        for k, at in enumerate(parts)
    ]


def best_kernel(own_ref, coverage_ref, c0, c1, c2, c3, partner_ref, best_ref, partner, turned, arrivals):
    rows, width = own_ref.shape
    scale = 1.0 / width**0.5
    copies = fetches(partner_ref, partner, arrivals)
    for copy in copies:
        copy.start()
    turned_table((c0, c1, c2, c3), turned)
    for t, table in enumerate((own_ref, partner)):
        for k, start in enumerate(range(0, rows, STEP)):
            if t == 1:
                copies[k].wait()
            sims = tile_sims(table, turned, start)
            top = functools.reduce(jnp.maximum, [sims[:, l : l + 128] for l in range(0, 512, 128)])
            for r in range(0, STEP, 128):
                here = pl.ds(start + r, 128)
                row = jnp.max(top[r : r + 128].T, axis=0, keepdims=True) * scale
                if t == 0:
                    row = jnp.maximum(row, coverage_ref[:, here])
                best_ref[t : t + 1, here] = row


def gain_kernel(cover_ref, turned, own_ref, partner_ref, gain_ref, own, partner, own_arrivals, arrivals):
    rows, width = own.shape
    scale = 1.0 / width**0.5
    copies = [fetches(own_ref, own, own_arrivals), fetches(partner_ref, partner, arrivals)]
    for copy in copies[0] + copies[1]:
        copy.start()
    total = jnp.zeros((8, 512), jnp.float32)
    for t, table in enumerate((own, partner)):
        for k, start in enumerate(range(0, rows, STEP)):
            copies[t][k].wait()
            sims = tile_sims(table, turned, start)
            for r in range(0, STEP, 128):
                line = cover_ref[t : t + 1, pl.ds(start + r, 128)] * width**0.5
                floor = jnp.broadcast_to(line, (128, 128)).T
                over = jnp.maximum(sims[r : r + 128] - jnp.concatenate([floor] * 4, axis=1), 0.0)
                total = total + jnp.sum(over.reshape(16, 8, 512), axis=0)
    sums = jnp.sum(total, axis=0, keepdims=True) * scale
    first = lax.axis_index("core") == 0
    x = lax.axis_index("x")
    yhi, ylo = lax.axis_index("yhi"), lax.axis_index("ylo")
    for late in range(4):
        for early in range(4):
            x_mask = jnp.where(first, early, late)
            y_mask = jnp.where(first, late, early)
            at = ((ylo ^ (y_mask & 1)) * 4 + (x ^ x_mask)) * 2 + (yhi ^ (y_mask >> 1))
            lane = late * 128 + early * 32
            gain_ref[pl.ds(at * 8, 8), :] = jnp.broadcast_to(sums[:, lane : lane + 32], (8, 32))


def on_chip(kernel, out, fetched, scratch, memory, *operands):
    rows, width = operands[-1].shape
    vmem = pl.BlockSpec(memory_space=pltpu.VMEM)
    return pl.pallas_call(
        kernel,
        out_shape=jax.ShapeDtypeStruct(out, jnp.float32),
        in_specs=[vmem] * (len(operands) - fetched) + [pl.BlockSpec(memory_space=pl.ANY)] * fetched,
        out_specs=vmem,
        scratch_shapes=[pltpu.VMEM((rows, width), jnp.bfloat16)] * fetched
        + scratch
        + [pltpu.SemaphoreType.DMA((rows // STEP,))] * fetched,
        compiler_params=pltpu.CompilerParams(vmem_limit_bytes=memory << 20),
        cost_estimate=pl.CostEstimate(flops=4096 * 512 * 768 * 2, bytes_accessed=8 << 20, transcendentals=0),
    )(*operands)


def pick_kernel(chosen_ref, cand_ref, table_ref, kept_ref, given_ref, found_ref, table, arrivals):
    rows, width = table.shape
    copies = fetches(table_ref, table, arrivals)
    for copy in copies:
        copy.start()
    core, yhi = lax.axis_index("core"), lax.axis_index("yhi")
    base = lax.axis_index(AXES) * rows

    lane = lax.broadcasted_iota(jnp.int32, (8, 128), 1)
    quarter = lane >> 5
    source = ((yhi ^ (quarter & 1)) << 6) | ((lane & 28) << 1) | ((core ^ (quarter >> 1)) << 2) | (lane & 3)
    wanted = jnp.take_along_axis(jnp.broadcast_to(cand_ref[...], (8, 128)), source, axis=1) - base
    wanted = jnp.broadcast_to(wanted[:1], (128, 128)).T

    left = chosen_ref[...] - base
    left = jnp.where((left >= 0) & (left < rows), left, rows).astype(jnp.float32)
    row = lax.broadcasted_iota(jnp.int32, (8, 128), 0)
    spots = jnp.full((8, 128), -1, jnp.int32)
    for s in range(MOST):
        least = jnp.min(jnp.min(left, axis=0, keepdims=True), axis=1, keepdims=True)
        left = jnp.where(left == least, float(rows), left)
        spots = jnp.where(row == s, least.astype(jnp.int32), spots)

    targets = jnp.concatenate([wanted, spots], axis=0)
    step = rows // len(copies)
    lanes = lax.broadcasted_iota(jnp.int32, (136, 128), 1)
    total = jnp.zeros((136, width), jnp.float32)
    for k, copy in enumerate(copies):
        hits = [targets == lanes + (k * step + l) for l in range(0, step, 128)]
        pick = jnp.concatenate([jnp.where(h, 1.0, 0.0).astype(jnp.bfloat16) for h in hits], axis=1)
        copy.wait()
        total = total + jnp.dot(pick, table[pl.ds(k * step, step), :], preferred_element_type=jnp.float32)
    kept_ref[...] = total[:64].astype(jnp.bfloat16)
    given_ref[...] = total[64:128].astype(jnp.bfloat16)
    found_ref[...] = total[128 : 128 + MOST].astype(jnp.bfloat16)


def settle_kernel(got_ref, block_ref):
    total = got_ref[0, :32, :].astype(jnp.float32)
    for z in range(1, 8):
        total = total + got_ref[z, :32, :].astype(jnp.float32)
    block_ref[:32, :] = total.astype(jnp.bfloat16)
    found = [got_ref[z, 32:, :].astype(jnp.float32) for z in range(8)]
    block_ref[32:, :] = jnp.concatenate(found, axis=0).astype(jnp.bfloat16)


def settled(got):
    vmem = pl.BlockSpec(memory_space=pltpu.VMEM)
    return pl.pallas_call(
        settle_kernel,
        out_shape=jax.ShapeDtypeStruct((64, got.shape[2]), jnp.bfloat16),
        in_specs=[vmem],
        out_specs=vmem,
        compiler_params=pltpu.CompilerParams(vmem_limit_bytes=8 << 20),
        cost_estimate=pl.CostEstimate(flops=1 << 20, bytes_accessed=1 << 20, transcendentals=0),
    )(got)


def own_picks(chosen_index, candidate_index, embeddings):
    rows, width = embeddings.shape
    vmem = pl.BlockSpec(memory_space=pltpu.VMEM)
    return pl.pallas_call(
        pick_kernel,
        out_shape=[jax.ShapeDtypeStruct((64, width), jnp.bfloat16)] * 2
        + [jax.ShapeDtypeStruct((MOST, width), jnp.bfloat16)],
        in_specs=[vmem, vmem, pl.BlockSpec(memory_space=pl.ANY)],
        out_specs=[vmem] * 3,
        scratch_shapes=[pltpu.VMEM((rows, width), jnp.bfloat16), pltpu.SemaphoreType.DMA((4,))],
        compiler_params=pltpu.CompilerParams(vmem_limit_bytes=60 << 20),
        cost_estimate=pl.CostEstimate(flops=136 * 2048 * 768 * 2, bytes_accessed=4 << 20, transcendentals=0),
    )(chosen_index.reshape(4, 128), candidate_index.reshape(1, 128), embeddings)


def local(embeddings, coverage, chosen_index, candidate_index):
    rows, width = embeddings.shape
    kept, given, found = own_picks(chosen_index, candidate_index, embeddings)
    half = kept + swap(given, 0, 1)
    half, later = lax.optimization_barrier((half, embeddings))
    partner = swap(later, 0, 1)
    quarter = half[:32] + swap(half[32:], 2, 0)
    send = jnp.concatenate([quarter, found], axis=0)
    got = lax.all_to_all(jnp.broadcast_to(send, (8, 32 + MOST, width)), "z", 0, 0)
    block = settled(got)
    line = jnp.stack([block] + [turn(block, s, True) for s in (1, 2, 3)])
    cands, chosen = line[:, :32].reshape(128, width), line[:, 32:].reshape(128, width)
    chosen = [chosen] + [turn(chosen, s, False) for s in (1, 2, 3)]
    cands = [cands] + [turn(cands, s, False) for s in (1, 2, 3)]

    best = on_chip(best_kernel, (2, rows), 1, [pltpu.VMEM((width, 512), jnp.bfloat16)], 24, embeddings, coverage.reshape(1, rows), *chosen, partner)
    turned = turned_pieces(cands)
    cover = jnp.maximum(best, swap(best, 0, 1)[::-1])
    part = on_chip(gain_kernel, (128, 32), 2, [], 52, cover, turned, embeddings, partner)
    parts = lax.all_to_all(part, CHIPS, 0, 0, tiled=True)
    gains = lax.dynamic_slice_in_dim(jnp.sum(parts, axis=0), lax.axis_index("z") * 4, 4)
    return cover[0], gains


def solution(mesh):
    torus = Mesh(mesh.devices.reshape(SIZES), AXES)
    return jax.shard_map(
        local,
        mesh=torus,
        in_specs=(P(AXES, None), P(AXES), P(), P(BLK)),
        out_specs=(P(AXES), P(AXES)),
        check_vma=False,
    )
```

```python
import functools

import jax
import jax.numpy as jnp
from jax import lax
from jax.experimental import pallas as pl
from jax.experimental.pallas import tpu as pltpu
from jax.sharding import Mesh
from jax.sharding import PartitionSpec as P

AXES = ("ylo", "x", "yhi", "z", "core")
SIZES = (2, 4, 2, 8, 2)
BLK = ("ylo", "x")
CHIPS = ("ylo", "x", "yhi", "z")
MOST = 4
STEP = 512


def place(y, x, z, core):
    return (((y % 2) * 4 + x) * 2 + y // 2) * 16 + z * 2 + core


def pairs_of(move):
    return [
        (place(y, x, z, core), place(*move(y, x, z, core)))
        for y in range(4)
        for x in range(4)
        for z in range(8)
        for core in range(2)
    ]


def swap(value, y_mask, core_mask):
    return lax.ppermute(value, AXES, pairs_of(lambda y, x, z, c: (y ^ y_mask, x, z, c ^ core_mask)))


def turn(value, mask, first):
    return lax.ppermute(
        value,
        AXES,
        pairs_of(lambda y, x, z, c: (y, x ^ mask, z, c) if (c == 0) == first else (y ^ mask, x, z, c)),
    )


def turned_table(pieces, turned):
    for k, piece in enumerate(pieces):
        turned[:, k * 128 : k * 128 + 128] = piece[...].T


def tile_sims(table, turned, start):
    return jnp.dot(table[pl.ds(start, STEP), :], turned[...], preferred_element_type=jnp.float32)


def turn_kernel(c0, c1, c2, c3, turned):
    turned_table((c0, c1, c2, c3), turned)


def turned_pieces(pieces):
    vmem = pl.BlockSpec(memory_space=pltpu.VMEM)
    return pl.pallas_call(
        turn_kernel,
        out_shape=jax.ShapeDtypeStruct((pieces[0].shape[1], 512), jnp.bfloat16),
        in_specs=[vmem] * 4,
        out_specs=vmem,
        compiler_params=pltpu.CompilerParams(vmem_limit_bytes=8 << 20),
        cost_estimate=pl.CostEstimate(flops=1 << 20, bytes_accessed=2 << 20, transcendentals=0),
    )(*pieces)


def fetches(source, target, arrivals):
    step = target.shape[0] // arrivals.shape[0]
    parts = [pl.ds(k * step, step) for k in range(arrivals.shape[0])]
    return [
        pltpu.make_async_copy(source.at[at, :], target.at[at, :], arrivals.at[k])
        for k, at in enumerate(parts)
    ]


def best_kernel(own_ref, coverage_ref, c0, c1, c2, c3, partner_ref, best_ref, turned):
    rows, width = own_ref.shape
    scale = 1.0 / width**0.5
    turned_table((c0, c1, c2, c3), turned)
    for t, table in enumerate((own_ref, partner_ref)):
        for start in range(0, rows, STEP):
            sims = tile_sims(table, turned, start)
            top = functools.reduce(jnp.maximum, [sims[:, l : l + 128] for l in range(0, 512, 128)])
            for r in range(0, STEP, 128):
                here = pl.ds(start + r, 128)
                row = jnp.max(top[r : r + 128].T, axis=0, keepdims=True) * scale
                if t == 0:
                    row = jnp.maximum(row, coverage_ref[:, here])
                best_ref[t : t + 1, here] = row


def gain_kernel(own_ref, best_ref, other_ref, turned, partner_ref, gain_ref, cover_ref):
    rows, width = own_ref.shape
    scale = 1.0 / width**0.5
    total = jnp.zeros((8, 512), jnp.float32)
    for t, table in enumerate((own_ref, partner_ref)):
        for start in range(0, rows, STEP):
            sims = tile_sims(table, turned, start)
            for r in range(0, STEP, 128):
                here = pl.ds(start + r, 128)
                line = jnp.maximum(best_ref[t : t + 1, here], other_ref[1 - t : 2 - t, here])
                if t == 0:
                    cover_ref[:, here] = line
                floor = jnp.broadcast_to(line * width**0.5, (128, 128)).T
                over = jnp.maximum(sims[r : r + 128] - jnp.concatenate([floor] * 4, axis=1), 0.0)
                total = total + jnp.sum(over.reshape(16, 8, 512), axis=0)
    sums = jnp.sum(total, axis=0, keepdims=True) * scale
    first = lax.axis_index("core") == 0
    x = lax.axis_index("x")
    yhi, ylo = lax.axis_index("yhi"), lax.axis_index("ylo")
    for late in range(4):
        for early in range(4):
            x_mask = jnp.where(first, early, late)
            y_mask = jnp.where(first, late, early)
            at = ((ylo ^ (y_mask & 1)) * 4 + (x ^ x_mask)) * 2 + (yhi ^ (y_mask >> 1))
            lane = late * 128 + early * 32
            gain_ref[pl.ds(at * 8, 8), :] = jnp.broadcast_to(sums[:, lane : lane + 32], (8, 32))


def on_chip(kernel, outs, scratch, *operands):
    vmem = pl.BlockSpec(memory_space=pltpu.VMEM)
    return pl.pallas_call(
        kernel,
        out_shape=[jax.ShapeDtypeStruct(out, jnp.float32) for out in outs],
        in_specs=[vmem] * len(operands),
        out_specs=[vmem] * len(outs),
        scratch_shapes=scratch,
        compiler_params=pltpu.CompilerParams(vmem_limit_bytes=16 << 20),
        cost_estimate=pl.CostEstimate(flops=4096 * 512 * 768 * 2, bytes_accessed=8 << 20, transcendentals=0),
    )(*operands)


def pick_kernel(chosen_ref, cand_ref, table_ref, kept_ref, given_ref, found_ref, table, arrivals):
    rows, width = table.shape
    copies = fetches(table_ref, table, arrivals)
    for copy in copies:
        copy.start()
    core, yhi = lax.axis_index("core"), lax.axis_index("yhi")
    base = lax.axis_index(AXES) * rows

    lane = lax.broadcasted_iota(jnp.int32, (8, 128), 1)
    quarter = lane >> 5
    source = ((yhi ^ (quarter & 1)) << 6) | ((lane & 28) << 1) | ((core ^ (quarter >> 1)) << 2) | (lane & 3)
    wanted = jnp.take_along_axis(jnp.broadcast_to(cand_ref[...], (8, 128)), source, axis=1) - base
    wanted = jnp.broadcast_to(wanted[:1], (128, 128)).T

    left = chosen_ref[...] - base
    left = jnp.where((left >= 0) & (left < rows), left, rows).astype(jnp.float32)
    row = lax.broadcasted_iota(jnp.int32, (8, 128), 0)
    spots = jnp.full((8, 128), -1, jnp.int32)
    for s in range(MOST):
        least = jnp.min(jnp.min(left, axis=0, keepdims=True), axis=1, keepdims=True)
        left = jnp.where(left == least, float(rows), left)
        spots = jnp.where(row == s, least.astype(jnp.int32), spots)

    targets = jnp.concatenate([wanted, spots], axis=0)
    step = rows // len(copies)
    lanes = lax.broadcasted_iota(jnp.int32, (136, 128), 1)
    total = jnp.zeros((136, width), jnp.float32)
    for k, copy in enumerate(copies):
        hits = [targets == lanes + (k * step + l) for l in range(0, step, 128)]
        pick = jnp.concatenate([jnp.where(h, 1.0, 0.0).astype(jnp.bfloat16) for h in hits], axis=1)
        copy.wait()
        total = total + jnp.dot(pick, table[pl.ds(k * step, step), :], preferred_element_type=jnp.float32)
    kept_ref[...] = total[:64].astype(jnp.bfloat16)
    given_ref[...] = total[64:128].astype(jnp.bfloat16)
    found_ref[...] = total[128 : 128 + MOST].astype(jnp.bfloat16)


def settle_kernel(got_ref, block_ref):
    total = got_ref[0, :32, :].astype(jnp.float32)
    for z in range(1, 8):
        total = total + got_ref[z, :32, :].astype(jnp.float32)
    block_ref[:32, :] = total.astype(jnp.bfloat16)
    found = [got_ref[z, 32:, :].astype(jnp.float32) for z in range(8)]
    block_ref[32:, :] = jnp.concatenate(found, axis=0).astype(jnp.bfloat16)


def settled(got):
    vmem = pl.BlockSpec(memory_space=pltpu.VMEM)
    return pl.pallas_call(
        settle_kernel,
        out_shape=jax.ShapeDtypeStruct((64, got.shape[2]), jnp.bfloat16),
        in_specs=[vmem],
        out_specs=vmem,
        compiler_params=pltpu.CompilerParams(vmem_limit_bytes=8 << 20),
        cost_estimate=pl.CostEstimate(flops=1 << 20, bytes_accessed=1 << 20, transcendentals=0),
    )(got)


def own_picks(chosen_index, candidate_index, embeddings):
    rows, width = embeddings.shape
    vmem = pl.BlockSpec(memory_space=pltpu.VMEM)
    return pl.pallas_call(
        pick_kernel,
        out_shape=[jax.ShapeDtypeStruct((64, width), jnp.bfloat16)] * 2
        + [jax.ShapeDtypeStruct((MOST, width), jnp.bfloat16)],
        in_specs=[vmem, vmem, pl.BlockSpec(memory_space=pl.ANY)],
        out_specs=[vmem] * 3,
        scratch_shapes=[pltpu.VMEM((rows, width), jnp.bfloat16), pltpu.SemaphoreType.DMA((4,))],
        compiler_params=pltpu.CompilerParams(vmem_limit_bytes=60 << 20),
        cost_estimate=pl.CostEstimate(flops=136 * 2048 * 768 * 2, bytes_accessed=4 << 20, transcendentals=0),
    )(chosen_index.reshape(4, 128), candidate_index.reshape(1, 128), embeddings)


def local(embeddings, coverage, chosen_index, candidate_index):
    rows, width = embeddings.shape
    kept, given, found = own_picks(chosen_index, candidate_index, embeddings)
    half = kept + swap(given, 0, 1)
    half, later = lax.optimization_barrier((half, embeddings))
    partner = swap(later, 0, 1)
    quarter = half[:32] + swap(half[32:], 2, 0)
    send = jnp.concatenate([quarter, found], axis=0)
    got = lax.all_to_all(jnp.broadcast_to(send, (8, 32 + MOST, width)), "z", 0, 0)
    block = settled(got)
    line = jnp.stack([block] + [turn(block, s, True) for s in (1, 2, 3)])
    cands, chosen = line[:, :32].reshape(128, width), line[:, 32:].reshape(128, width)
    chosen = [chosen] + [turn(chosen, s, False) for s in (1, 2, 3)]
    cands = [cands] + [turn(cands, s, False) for s in (1, 2, 3)]

    table = [pltpu.VMEM((width, 512), jnp.bfloat16)]
    best = on_chip(best_kernel, [(2, rows)], table, embeddings, coverage.reshape(1, rows), *chosen, partner)[0]
    other = swap(best, 0, 1)
    turned = turned_pieces(cands)
    part, cover = on_chip(gain_kernel, [(128, 32), (1, rows)], [], embeddings, best, other, turned, partner)
    parts = lax.all_to_all(part, CHIPS, 0, 0, tiled=True)
    gains = lax.dynamic_slice_in_dim(jnp.sum(parts, axis=0), lax.axis_index("z") * 4, 4)
    return cover[0], gains


def solution(mesh):
    torus = Mesh(mesh.devices.reshape(SIZES), AXES)
    return jax.shard_map(
        local,
        mesh=torus,
        in_specs=(P(AXES, None), P(AXES), P(), P(BLK)),
        out_specs=(P(AXES), P(AXES)),
        check_vma=False,
    )
```

```python
import functools

import jax
import jax.numpy as jnp
from jax import lax
from jax.experimental import pallas as pl
from jax.experimental.pallas import tpu as pltpu
from jax.sharding import Mesh
from jax.sharding import PartitionSpec as P

AXES = ("ylo", "x", "yhi", "z", "core")
SIZES = (2, 4, 2, 8, 2)
BLK = ("ylo", "x")
CHIPS = ("ylo", "x", "yhi", "z")
MOST = 4
STEP = 512


def place(y, x, z, core):
    return (((y % 2) * 4 + x) * 2 + y // 2) * 16 + z * 2 + core


def pairs_of(move):
    return [
        (place(y, x, z, core), place(*move(y, x, z, core)))
        for y in range(4)
        for x in range(4)
        for z in range(8)
        for core in range(2)
    ]


def swap(value, y_mask, core_mask):
    return lax.ppermute(value, AXES, pairs_of(lambda y, x, z, c: (y ^ y_mask, x, z, c ^ core_mask)))


def turn(value, mask, first):
    return lax.ppermute(
        value,
        AXES,
        pairs_of(lambda y, x, z, c: (y, x ^ mask, z, c) if (c == 0) == first else (y ^ mask, x, z, c)),
    )


def turned_table(pieces, turned):
    for k, piece in enumerate(pieces):
        turned[:, k * 128 : k * 128 + 128] = piece[...].T


def tile_sims(table, turned, start):
    return jnp.dot(table[pl.ds(start, STEP), :], turned[...], preferred_element_type=jnp.float32)


def turn_kernel(c0, c1, c2, c3, turned):
    turned_table((c0, c1, c2, c3), turned)


def turned_pieces(pieces):
    vmem = pl.BlockSpec(memory_space=pltpu.VMEM)
    return pl.pallas_call(
        turn_kernel,
        out_shape=jax.ShapeDtypeStruct((pieces[0].shape[1], 512), jnp.bfloat16),
        in_specs=[vmem] * 4,
        out_specs=vmem,
        compiler_params=pltpu.CompilerParams(vmem_limit_bytes=8 << 20),
        cost_estimate=pl.CostEstimate(flops=1 << 20, bytes_accessed=2 << 20, transcendentals=0),
    )(*pieces)


def best_kernel(own_ref, coverage_ref, c0, c1, c2, c3, partner_ref, best_ref, turned):
    rows, width = own_ref.shape
    scale = 1.0 / width**0.5
    turned_table((c0, c1, c2, c3), turned)
    for t, table in enumerate((own_ref, partner_ref)):
        for start in range(0, rows, STEP):
            sims = tile_sims(table, turned, start)
            top = functools.reduce(jnp.maximum, [sims[:, l : l + 128] for l in range(0, 512, 128)])
            for r in range(0, STEP, 128):
                here = pl.ds(start + r, 128)
                row = jnp.max(top[r : r + 128].T, axis=0, keepdims=True) * scale
                if t == 0:
                    row = jnp.maximum(row, coverage_ref[:, here])
                best_ref[t : t + 1, here] = row


def gain_kernel(own_ref, best_ref, other_ref, turned, partner_ref, gain_ref, cover_ref):
    rows, width = own_ref.shape
    scale = 1.0 / width**0.5
    total = jnp.zeros((8, 512), jnp.float32)
    for t, table in enumerate((own_ref, partner_ref)):
        for start in range(0, rows, STEP):
            sims = tile_sims(table, turned, start)
            for r in range(0, STEP, 128):
                here = pl.ds(start + r, 128)
                line = jnp.maximum(best_ref[t : t + 1, here], other_ref[1 - t : 2 - t, here])
                if t == 0:
                    cover_ref[:, here] = line
                floor = jnp.broadcast_to(line * width**0.5, (128, 128)).T
                over = jnp.maximum(sims[r : r + 128] - jnp.concatenate([floor] * 4, axis=1), 0.0)
                total = total + jnp.sum(over.reshape(16, 8, 512), axis=0)
    sums = jnp.sum(total, axis=0, keepdims=True) * scale
    first = lax.axis_index("core") == 0
    x = lax.axis_index("x")
    yhi, ylo = lax.axis_index("yhi"), lax.axis_index("ylo")
    for late in range(4):
        for early in range(4):
            x_mask = jnp.where(first, early, late)
            y_mask = jnp.where(first, late, early)
            at = ((ylo ^ (y_mask & 1)) * 4 + (x ^ x_mask)) * 2 + (yhi ^ (y_mask >> 1))
            lane = late * 128 + early * 32
            gain_ref[pl.ds(at * 8, 8), :] = jnp.broadcast_to(sums[:, lane : lane + 32], (8, 32))


def on_chip(kernel, outs, scratch, *operands):
    vmem = pl.BlockSpec(memory_space=pltpu.VMEM)
    return pl.pallas_call(
        kernel,
        out_shape=[jax.ShapeDtypeStruct(out, jnp.float32) for out in outs],
        in_specs=[vmem] * len(operands),
        out_specs=[vmem] * len(outs),
        scratch_shapes=scratch,
        compiler_params=pltpu.CompilerParams(vmem_limit_bytes=16 << 20),
        cost_estimate=pl.CostEstimate(flops=4096 * 512 * 768 * 2, bytes_accessed=8 << 20, transcendentals=0),
    )(*operands)


def pick_kernel(chosen_ref, cand_ref, table, kept_ref, given_ref, found_ref):
    rows, width = table.shape
    core, yhi = lax.axis_index("core"), lax.axis_index("yhi")
    base = lax.axis_index(AXES) * rows

    lane = lax.broadcasted_iota(jnp.int32, (8, 128), 1)
    quarter = lane >> 5
    source = ((yhi ^ (quarter & 1)) << 6) | ((lane & 28) << 1) | ((core ^ (quarter >> 1)) << 2) | (lane & 3)
    wanted = jnp.take_along_axis(jnp.broadcast_to(cand_ref[...], (8, 128)), source, axis=1) - base
    wanted = jnp.broadcast_to(wanted[:1], (128, 128)).T

    left = chosen_ref[...] - base
    left = jnp.where((left >= 0) & (left < rows), left, rows).astype(jnp.float32)
    row = lax.broadcasted_iota(jnp.int32, (8, 128), 0)
    spots = jnp.full((8, 128), -1, jnp.int32)
    for s in range(MOST):
        least = jnp.min(jnp.min(left, axis=0, keepdims=True), axis=1, keepdims=True)
        left = jnp.where(left == least, float(rows), left)
        spots = jnp.where(row == s, least.astype(jnp.int32), spots)

    targets = jnp.concatenate([wanted, spots], axis=0)
    step = 512
    lanes = lax.broadcasted_iota(jnp.int32, (136, 128), 1)
    total = jnp.zeros((136, width), jnp.float32)
    for k in range(rows // step):
        hits = [targets == lanes + (k * step + l) for l in range(0, step, 128)]
        pick = jnp.concatenate([jnp.where(h, 1.0, 0.0).astype(jnp.bfloat16) for h in hits], axis=1)
        total = total + jnp.dot(pick, table[pl.ds(k * step, step), :], preferred_element_type=jnp.float32)
    kept_ref[...] = total[:64].astype(jnp.bfloat16)
    given_ref[...] = total[64:128].astype(jnp.bfloat16)
    found_ref[...] = total[128 : 128 + MOST].astype(jnp.bfloat16)


def settle_kernel(got_ref, block_ref):
    total = got_ref[0, :32, :].astype(jnp.float32)
    for z in range(1, 8):
        total = total + got_ref[z, :32, :].astype(jnp.float32)
    block_ref[:32, :] = total.astype(jnp.bfloat16)
    found = [got_ref[z, 32:, :].astype(jnp.float32) for z in range(8)]
    block_ref[32:, :] = jnp.concatenate(found, axis=0).astype(jnp.bfloat16)


def settled(got):
    vmem = pl.BlockSpec(memory_space=pltpu.VMEM)
    return pl.pallas_call(
        settle_kernel,
        out_shape=jax.ShapeDtypeStruct((64, got.shape[2]), jnp.bfloat16),
        in_specs=[vmem],
        out_specs=vmem,
        compiler_params=pltpu.CompilerParams(vmem_limit_bytes=8 << 20),
        cost_estimate=pl.CostEstimate(flops=1 << 20, bytes_accessed=1 << 20, transcendentals=0),
    )(got)


def own_picks(chosen_index, candidate_index, embeddings):
    rows, width = embeddings.shape
    vmem = pl.BlockSpec(memory_space=pltpu.VMEM)
    return pl.pallas_call(
        pick_kernel,
        out_shape=[jax.ShapeDtypeStruct((64, width), jnp.bfloat16)] * 2
        + [jax.ShapeDtypeStruct((MOST, width), jnp.bfloat16)],
        in_specs=[vmem] * 3,
        out_specs=[vmem] * 3,
        compiler_params=pltpu.CompilerParams(vmem_limit_bytes=40 << 20),
        cost_estimate=pl.CostEstimate(flops=136 * 2048 * 768 * 2, bytes_accessed=4 << 20, transcendentals=0),
    )(chosen_index.reshape(4, 128), candidate_index.reshape(1, 128), embeddings)


def local(embeddings, coverage, chosen_index, candidate_index):
    rows, width = embeddings.shape
    kept, given, found = own_picks(chosen_index, candidate_index, embeddings)
    half = kept + swap(given, 0, 1)
    half, later = lax.optimization_barrier((half, embeddings))
    partner = swap(later, 0, 1)
    quarter = half[:32] + swap(half[32:], 2, 0)
    send = jnp.concatenate([quarter, found], axis=0)
    got = lax.all_to_all(jnp.broadcast_to(send, (8, 32 + MOST, width)), "z", 0, 0)
    block = settled(got)
    line = jnp.stack([block] + [turn(block, s, True) for s in (1, 2, 3)])
    cands, chosen = line[:, :32].reshape(128, width), line[:, 32:].reshape(128, width)
    chosen = [chosen] + [turn(chosen, s, False) for s in (1, 2, 3)]
    cands = [cands] + [turn(cands, s, False) for s in (1, 2, 3)]

    table = [pltpu.VMEM((width, 512), jnp.bfloat16)]
    best = on_chip(best_kernel, [(2, rows)], table, embeddings, coverage.reshape(1, rows), *chosen, partner)[0]
    other = swap(best, 0, 1)
    turned = turned_pieces(cands)
    part, cover = on_chip(gain_kernel, [(128, 32), (1, rows)], [], embeddings, best, other, turned, partner)
    parts = lax.all_to_all(part, CHIPS, 0, 0, tiled=True)
    gains = lax.dynamic_slice_in_dim(jnp.sum(parts, axis=0), lax.axis_index("z") * 4, 4)
    return cover[0], gains


def solution(mesh):
    torus = Mesh(mesh.devices.reshape(SIZES), AXES)
    return jax.shard_map(
        local,
        mesh=torus,
        in_specs=(P(AXES, None), P(AXES), P(), P(BLK)),
        out_specs=(P(AXES), P(AXES)),
        check_vma=False,
    )
```

```python
import functools

import jax
import jax.numpy as jnp
from jax import lax
from jax.experimental import pallas as pl
from jax.experimental.pallas import tpu as pltpu
from jax.sharding import Mesh
from jax.sharding import PartitionSpec as P

AXES = ("ylo", "x", "yhi", "z", "core")
SIZES = (2, 4, 2, 8, 2)
BLK = ("ylo", "x")
CHIPS = ("ylo", "x", "yhi", "z")
MOST = 4
STEP = 512


def place(y, x, z, core):
    return (((y % 2) * 4 + x) * 2 + y // 2) * 16 + z * 2 + core


def pairs_of(move):
    return [
        (place(y, x, z, core), place(*move(y, x, z, core)))
        for y in range(4)
        for x in range(4)
        for z in range(8)
        for core in range(2)
    ]


def swap(value, y_mask, core_mask):
    return lax.ppermute(value, AXES, pairs_of(lambda y, x, z, c: (y ^ y_mask, x, z, c ^ core_mask)))


def turn(value, mask, first):
    return lax.ppermute(
        value,
        AXES,
        pairs_of(lambda y, x, z, c: (y, x ^ mask, z, c) if (c == 0) == first else (y ^ mask, x, z, c)),
    )


def turned_table(pieces, turned):
    for k, piece in enumerate(pieces):
        turned[:, k * 128 : k * 128 + 128] = piece[...].T


def tile_sims(table, turned, start):
    return jnp.dot(table[pl.ds(start, STEP), :], turned[...], preferred_element_type=jnp.float32)


def turn_kernel(c0, c1, c2, c3, turned):
    turned_table((c0, c1, c2, c3), turned)


def turned_pieces(pieces):
    vmem = pl.BlockSpec(memory_space=pltpu.VMEM)
    return pl.pallas_call(
        turn_kernel,
        out_shape=jax.ShapeDtypeStruct((pieces[0].shape[1], 512), jnp.bfloat16),
        in_specs=[vmem] * 4,
        out_specs=vmem,
        compiler_params=pltpu.CompilerParams(vmem_limit_bytes=8 << 20),
        cost_estimate=pl.CostEstimate(flops=1 << 20, bytes_accessed=2 << 20, transcendentals=0),
    )(*pieces)


def best_kernel(own_ref, coverage_ref, c0, c1, c2, c3, partner_ref, best_ref, turned):
    rows, width = own_ref.shape
    scale = 1.0 / width**0.5
    turned_table((c0, c1, c2, c3), turned)
    for t, table in enumerate((own_ref, partner_ref)):
        for start in range(0, rows, STEP):
            sims = tile_sims(table, turned, start)
            top = functools.reduce(jnp.maximum, [sims[:, l : l + 128] for l in range(0, 512, 128)])
            for r in range(0, STEP, 128):
                here = pl.ds(start + r, 128)
                row = jnp.max(top[r : r + 128].T, axis=0, keepdims=True) * scale
                if t == 0:
                    row = jnp.maximum(row, coverage_ref[:, here])
                best_ref[t : t + 1, here] = row


def gain_kernel(own_ref, best_ref, other_ref, turned, partner_ref, gain_ref, cover_ref):
    rows, width = own_ref.shape
    scale = 1.0 / width**0.5
    total = jnp.zeros((8, 512), jnp.float32)
    for t, table in enumerate((own_ref, partner_ref)):
        for start in range(0, rows, STEP):
            sims = tile_sims(table, turned, start)
            for r in range(0, STEP, 128):
                here = pl.ds(start + r, 128)
                line = jnp.maximum(best_ref[t : t + 1, here], other_ref[1 - t : 2 - t, here])
                if t == 0:
                    cover_ref[:, here] = line
                floor = jnp.broadcast_to(line * width**0.5, (128, 128)).T
                over = jnp.maximum(sims[r : r + 128] - jnp.concatenate([floor] * 4, axis=1), 0.0)
                total = total + jnp.sum(over.reshape(16, 8, 512), axis=0)
    sums = jnp.sum(total, axis=0, keepdims=True) * scale
    first = lax.axis_index("core") == 0
    x = lax.axis_index("x")
    yhi, ylo = lax.axis_index("yhi"), lax.axis_index("ylo")
    for late in range(4):
        for early in range(4):
            x_mask = jnp.where(first, early, late)
            y_mask = jnp.where(first, late, early)
            at = ((ylo ^ (y_mask & 1)) * 4 + (x ^ x_mask)) * 2 + (yhi ^ (y_mask >> 1))
            lane = late * 128 + early * 32
            gain_ref[pl.ds(at * 8, 8), :] = jnp.broadcast_to(sums[:, lane : lane + 32], (8, 32))


def on_chip(kernel, outs, scratch, *operands):
    vmem = pl.BlockSpec(memory_space=pltpu.VMEM)
    return pl.pallas_call(
        kernel,
        out_shape=[jax.ShapeDtypeStruct(out, jnp.float32) for out in outs],
        in_specs=[vmem] * len(operands),
        out_specs=[vmem] * len(outs),
        scratch_shapes=scratch,
        compiler_params=pltpu.CompilerParams(vmem_limit_bytes=16 << 20),
        cost_estimate=pl.CostEstimate(flops=4096 * 512 * 768 * 2, bytes_accessed=8 << 20, transcendentals=0),
    )(*operands)


def spot_kernel(rows, index_ref, targets_ref):
    core, yhi = lax.axis_index("core"), lax.axis_index("yhi")
    base = lax.axis_index(AXES) * rows

    lane = lax.broadcasted_iota(jnp.int32, (8, 128), 1)
    quarter = lane >> 5
    source = ((yhi ^ (quarter & 1)) << 6) | ((lane & 28) << 1) | ((core ^ (quarter >> 1)) << 2) | (lane & 3)
    wanted = jnp.take_along_axis(jnp.broadcast_to(index_ref[4:5, :], (8, 128)), source, axis=1) - base
    wanted = jnp.broadcast_to(wanted[:1], (128, 128)).T

    left = index_ref[:4, :] - base
    left = jnp.where((left >= 0) & (left < rows), left, rows).astype(jnp.float32)
    row = lax.broadcasted_iota(jnp.int32, (8, 128), 0)
    spots = jnp.full((8, 128), -1, jnp.int32)
    for s in range(MOST):
        least = jnp.min(jnp.min(left, axis=0, keepdims=True), axis=1, keepdims=True)
        left = jnp.where(left == least, float(rows), left)
        spots = jnp.where(row == s, least.astype(jnp.int32), spots)

    targets_ref[:128, :] = wanted
    targets_ref[128:, :] = spots


def pick_kernel(targets_ref, table, kept_ref, given_ref, found_ref):
    rows, width = table.shape
    targets = targets_ref[...]
    step = 512
    lanes = lax.broadcasted_iota(jnp.int32, (136, 128), 1)
    total = jnp.zeros((136, width), jnp.float32)
    for k in range(rows // step):
        hits = [targets == lanes + (k * step + l) for l in range(0, step, 128)]
        pick = jnp.concatenate([jnp.where(h, 1.0, 0.0).astype(jnp.bfloat16) for h in hits], axis=1)
        total = total + jnp.dot(pick, table[pl.ds(k * step, step), :], preferred_element_type=jnp.float32)
    kept_ref[...] = total[:64].astype(jnp.bfloat16)
    given_ref[...] = total[64:128].astype(jnp.bfloat16)
    found_ref[...] = total[128 : 128 + MOST].astype(jnp.bfloat16)


def settle_kernel(got_ref, block_ref):
    total = got_ref[0, :32, :].astype(jnp.float32)
    for z in range(1, 8):
        total = total + got_ref[z, :32, :].astype(jnp.float32)
    block_ref[:32, :] = total.astype(jnp.bfloat16)
    found = [got_ref[z, 32:, :].astype(jnp.float32) for z in range(8)]
    block_ref[32:, :] = jnp.concatenate(found, axis=0).astype(jnp.bfloat16)


def settled(got):
    vmem = pl.BlockSpec(memory_space=pltpu.VMEM)
    return pl.pallas_call(
        settle_kernel,
        out_shape=jax.ShapeDtypeStruct((64, got.shape[2]), jnp.bfloat16),
        in_specs=[vmem],
        out_specs=vmem,
        compiler_params=pltpu.CompilerParams(vmem_limit_bytes=8 << 20),
        cost_estimate=pl.CostEstimate(flops=1 << 20, bytes_accessed=1 << 20, transcendentals=0),
    )(got)


def own_picks(chosen_index, candidate_index, embeddings):
    rows, width = embeddings.shape
    index = jnp.concatenate([chosen_index, candidate_index]).reshape(5, 128)
    vmem = pl.BlockSpec(memory_space=pltpu.VMEM)
    targets = pl.pallas_call(
        functools.partial(spot_kernel, rows),
        out_shape=jax.ShapeDtypeStruct((136, 128), jnp.int32),
        in_specs=[vmem],
        out_specs=vmem,
        compiler_params=pltpu.CompilerParams(vmem_limit_bytes=8 << 20),
        cost_estimate=pl.CostEstimate(flops=1 << 32, bytes_accessed=1 << 17, transcendentals=0),
    )(index)
    return pl.pallas_call(
        pick_kernel,
        out_shape=[jax.ShapeDtypeStruct((64, width), jnp.bfloat16)] * 2
        + [jax.ShapeDtypeStruct((MOST, width), jnp.bfloat16)],
        in_specs=[vmem] * 2,
        out_specs=[vmem] * 3,
        compiler_params=pltpu.CompilerParams(vmem_limit_bytes=40 << 20),
        cost_estimate=pl.CostEstimate(flops=136 * 2048 * 768 * 2, bytes_accessed=4 << 20, transcendentals=0),
    )(targets, embeddings)


def local(embeddings, coverage, chosen_index, candidate_index):
    rows, width = embeddings.shape
    kept, given, found = own_picks(chosen_index, candidate_index, embeddings)
    half = kept + swap(given, 0, 1)
    half, later = lax.optimization_barrier((half, embeddings))
    partner = swap(later, 0, 1)
    quarter = half[:32] + swap(half[32:], 2, 0)
    send = jnp.concatenate([quarter, found], axis=0)
    got = lax.all_to_all(jnp.broadcast_to(send, (8, 32 + MOST, width)), "z", 0, 0)
    block = settled(got)
    line = jnp.stack([block] + [turn(block, s, True) for s in (1, 2, 3)])
    cands, chosen = line[:, :32].reshape(128, width), line[:, 32:].reshape(128, width)
    chosen = [chosen] + [turn(chosen, s, False) for s in (1, 2, 3)]
    cands = [cands] + [turn(cands, s, False) for s in (1, 2, 3)]

    table = [pltpu.VMEM((width, 512), jnp.bfloat16)]
    best = on_chip(best_kernel, [(2, rows)], table, embeddings, coverage.reshape(1, rows), *chosen, partner)[0]
    other = swap(best, 0, 1)
    turned = turned_pieces(cands)
    part, cover = on_chip(gain_kernel, [(128, 32), (1, rows)], [], embeddings, best, other, turned, partner)
    parts = lax.all_to_all(part, CHIPS, 0, 0, tiled=True)
    gains = jnp.sum(lax.dynamic_slice_in_dim(parts, lax.axis_index("z") * 4, 4, 1), axis=0)
    return cover[0], gains


def solution(mesh):
    torus = Mesh(mesh.devices.reshape(SIZES), AXES)
    return jax.shard_map(
        local,
        mesh=torus,
        in_specs=(P(AXES, None), P(AXES), P(), P(BLK)),
        out_specs=(P(AXES), P(AXES)),
        check_vma=False,
    )
```

```python
import functools

import jax
import jax.numpy as jnp
from jax import lax
from jax.experimental import pallas as pl
from jax.experimental.pallas import tpu as pltpu
from jax.sharding import Mesh
from jax.sharding import PartitionSpec as P

AXES = ("ylo", "x", "yhi", "z", "core")
SIZES = (2, 4, 2, 8, 2)
BLK = ("ylo", "x")
CHIPS = ("ylo", "x", "yhi", "z")
MOST = 4
STEP = 512


def place(y, x, z, core):
    return (((y % 2) * 4 + x) * 2 + y // 2) * 16 + z * 2 + core


def pairs_of(move):
    return [
        (place(y, x, z, core), place(*move(y, x, z, core)))
        for y in range(4)
        for x in range(4)
        for z in range(8)
        for core in range(2)
    ]


def swap(value, y_mask, core_mask):
    return lax.ppermute(value, AXES, pairs_of(lambda y, x, z, c: (y ^ y_mask, x, z, c ^ core_mask)))


def turn(value, mask, first):
    return lax.ppermute(
        value,
        AXES,
        pairs_of(lambda y, x, z, c: (y, x ^ mask, z, c) if (c == 0) == first else (y ^ mask, x, z, c)),
    )


def turned_table(pieces, turned):
    for k, piece in enumerate(pieces):
        turned[:, k * 128 : k * 128 + 128] = piece[...].T


def tile_sims(table, turned, start):
    return jnp.dot(table[pl.ds(start, STEP), :], turned[...], preferred_element_type=jnp.float32)


def turn_kernel(c0, c1, c2, c3, turned):
    turned_table((c0, c1, c2, c3), turned)


def turned_pieces(pieces):
    vmem = pl.BlockSpec(memory_space=pltpu.VMEM)
    return pl.pallas_call(
        turn_kernel,
        out_shape=jax.ShapeDtypeStruct((pieces[0].shape[1], 512), jnp.bfloat16),
        in_specs=[vmem] * 4,
        out_specs=vmem,
        compiler_params=pltpu.CompilerParams(vmem_limit_bytes=8 << 20),
        cost_estimate=pl.CostEstimate(flops=1 << 20, bytes_accessed=2 << 20, transcendentals=0),
    )(*pieces)


def best_kernel(own_ref, floor_ref, c0, c1, partner_ref, best_ref, turned):
    rows, width = own_ref.shape
    scale = 1.0 / width**0.5
    turned_table((c0, c1), turned)
    for t, table in enumerate((own_ref, partner_ref)):
        for start in range(0, rows, STEP):
            sims = tile_sims(table, turned, start)
            top = functools.reduce(jnp.maximum, [sims[:, l : l + 128] for l in range(0, 256, 128)])
            for r in range(0, STEP, 128):
                here = pl.ds(start + r, 128)
                row = jnp.max(top[r : r + 128].T, axis=0, keepdims=True) * scale
                if t < floor_ref.shape[0]:
                    row = jnp.maximum(row, floor_ref[t : t + 1, here])
                best_ref[t : t + 1, here] = row


def gain_kernel(own_ref, best_ref, other_ref, turned, partner_ref, gain_ref, cover_ref):
    rows, width = own_ref.shape
    scale = 1.0 / width**0.5
    total = jnp.zeros((8, 512), jnp.float32)
    for t, table in enumerate((own_ref, partner_ref)):
        for start in range(0, rows, STEP):
            sims = tile_sims(table, turned, start)
            for r in range(0, STEP, 128):
                here = pl.ds(start + r, 128)
                line = jnp.maximum(best_ref[t : t + 1, here], other_ref[1 - t : 2 - t, here])
                if t == 0:
                    cover_ref[:, here] = line
                floor = jnp.broadcast_to(line * width**0.5, (128, 128)).T
                over = jnp.maximum(sims[r : r + 128] - jnp.concatenate([floor] * 4, axis=1), 0.0)
                total = total + jnp.sum(over.reshape(16, 8, 512), axis=0)
    sums = jnp.sum(total, axis=0, keepdims=True) * scale
    first = lax.axis_index("core") == 0
    x = lax.axis_index("x")
    yhi, ylo = lax.axis_index("yhi"), lax.axis_index("ylo")
    for late in range(4):
        for early in range(4):
            x_mask = jnp.where(first, early, late)
            y_mask = jnp.where(first, late, early)
            at = ((ylo ^ (y_mask & 1)) * 4 + (x ^ x_mask)) * 2 + (yhi ^ (y_mask >> 1))
            lane = late * 128 + early * 32
            gain_ref[pl.ds(at * 8, 8), :] = jnp.broadcast_to(sums[:, lane : lane + 32], (8, 32))


def on_chip(kernel, outs, scratch, pieces, *operands):
    vmem = pl.BlockSpec(memory_space=pltpu.VMEM)
    return pl.pallas_call(
        kernel,
        out_shape=[jax.ShapeDtypeStruct(out, jnp.float32) for out in outs],
        in_specs=[vmem] * len(operands),
        out_specs=[vmem] * len(outs),
        scratch_shapes=scratch,
        compiler_params=pltpu.CompilerParams(vmem_limit_bytes=16 << 20),
        cost_estimate=pl.CostEstimate(flops=4096 * 128 * 768 * 2 * pieces, bytes_accessed=8 << 20, transcendentals=0),
    )(*operands)


def spot_kernel(rows, index_ref, targets_ref):
    core, yhi = lax.axis_index("core"), lax.axis_index("yhi")
    base = lax.axis_index(AXES) * rows

    lane = lax.broadcasted_iota(jnp.int32, (8, 128), 1)
    quarter = lane >> 5
    source = ((yhi ^ (quarter & 1)) << 6) | ((lane & 28) << 1) | ((core ^ (quarter >> 1)) << 2) | (lane & 3)
    wanted = jnp.take_along_axis(jnp.broadcast_to(index_ref[4:5, :], (8, 128)), source, axis=1) - base
    wanted = jnp.broadcast_to(wanted[:1], (128, 128)).T

    left = index_ref[:4, :] - base
    left = jnp.where((left >= 0) & (left < rows), left, rows).astype(jnp.float32)
    row = lax.broadcasted_iota(jnp.int32, (8, 128), 0)
    spots = jnp.full((8, 128), -1, jnp.int32)
    for s in range(MOST):
        least = jnp.min(jnp.min(left, axis=0, keepdims=True), axis=1, keepdims=True)
        left = jnp.where(left == least, float(rows), left)
        spots = jnp.where(row == s, least.astype(jnp.int32), spots)

    targets_ref[:128, :] = wanted
    targets_ref[128:, :] = spots


def pick_kernel(targets_ref, table, kept_ref, given_ref, found_ref):
    rows, width = table.shape
    targets = targets_ref[...]
    step = 512
    lanes = lax.broadcasted_iota(jnp.int32, (136, 128), 1)
    total = jnp.zeros((136, width), jnp.float32)
    for k in range(rows // step):
        hits = [targets == lanes + (k * step + l) for l in range(0, step, 128)]
        pick = jnp.concatenate([jnp.where(h, 1.0, 0.0).astype(jnp.bfloat16) for h in hits], axis=1)
        total = total + jnp.dot(pick, table[pl.ds(k * step, step), :], preferred_element_type=jnp.float32)
    kept_ref[...] = total[:64].astype(jnp.bfloat16)
    given_ref[...] = total[64:128].astype(jnp.bfloat16)
    found_ref[...] = total[128 : 128 + MOST].astype(jnp.bfloat16)


def settle_kernel(got_ref, block_ref):
    total = got_ref[0, :32, :].astype(jnp.float32)
    for z in range(1, 8):
        total = total + got_ref[z, :32, :].astype(jnp.float32)
    block_ref[:32, :] = total.astype(jnp.bfloat16)
    found = [got_ref[z, 32:, :].astype(jnp.float32) for z in range(8)]
    block_ref[32:, :] = jnp.concatenate(found, axis=0).astype(jnp.bfloat16)


def settled(got):
    vmem = pl.BlockSpec(memory_space=pltpu.VMEM)
    return pl.pallas_call(
        settle_kernel,
        out_shape=jax.ShapeDtypeStruct((64, got.shape[2]), jnp.bfloat16),
        in_specs=[vmem],
        out_specs=vmem,
        compiler_params=pltpu.CompilerParams(vmem_limit_bytes=8 << 20),
        cost_estimate=pl.CostEstimate(flops=1 << 20, bytes_accessed=1 << 20, transcendentals=0),
    )(got)


def own_picks(chosen_index, candidate_index, embeddings):
    rows, width = embeddings.shape
    index = jnp.concatenate([chosen_index, candidate_index]).reshape(5, 128)
    vmem = pl.BlockSpec(memory_space=pltpu.VMEM)
    targets = pl.pallas_call(
        functools.partial(spot_kernel, rows),
        out_shape=jax.ShapeDtypeStruct((136, 128), jnp.int32),
        in_specs=[vmem],
        out_specs=vmem,
        compiler_params=pltpu.CompilerParams(vmem_limit_bytes=8 << 20),
        cost_estimate=pl.CostEstimate(flops=1 << 32, bytes_accessed=1 << 17, transcendentals=0),
    )(index)
    return pl.pallas_call(
        pick_kernel,
        out_shape=[jax.ShapeDtypeStruct((64, width), jnp.bfloat16)] * 2
        + [jax.ShapeDtypeStruct((MOST, width), jnp.bfloat16)],
        in_specs=[vmem] * 2,
        out_specs=[vmem] * 3,
        compiler_params=pltpu.CompilerParams(vmem_limit_bytes=40 << 20),
        cost_estimate=pl.CostEstimate(flops=136 * 2048 * 768 * 2, bytes_accessed=4 << 20, transcendentals=0),
    )(targets, embeddings)


def local(embeddings, coverage, chosen_index, candidate_index):
    rows, width = embeddings.shape
    kept, given, found = own_picks(chosen_index, candidate_index, embeddings)
    half = kept + swap(given, 0, 1)
    half, later = lax.optimization_barrier((half, embeddings))
    partner = swap(later, 0, 1)
    quarter = half[:32] + swap(half[32:], 2, 0)
    send = jnp.concatenate([quarter, found], axis=0)
    got = lax.all_to_all(jnp.broadcast_to(send, (8, 32 + MOST, width)), "z", 0, 0)
    block = settled(got)
    line = jnp.stack([block] + [turn(block, s, True) for s in (1, 2, 3)])
    cands, chosen = line[:, :32].reshape(128, width), line[:, 32:].reshape(128, width)
    chosen = [chosen] + [turn(chosen, s, False) for s in (1, 2, 3)]
    cands = [cands] + [turn(cands, s, False) for s in (1, 2, 3)]

    table = [pltpu.VMEM((width, 256), jnp.bfloat16)]
    best = coverage.reshape(1, rows)
    for pieces in (chosen[:2], chosen[2:]):
        best = on_chip(best_kernel, [(2, rows)], table, 2, embeddings, best, *pieces, partner)[0]
    other = swap(best, 0, 1)
    turned = turned_pieces(cands)
    part, cover = on_chip(gain_kernel, [(128, 32), (1, rows)], [], 4, embeddings, best, other, turned, partner)
    parts = lax.all_to_all(part, CHIPS, 0, 0, tiled=True)
    gains = jnp.sum(lax.dynamic_slice_in_dim(parts, lax.axis_index("z") * 4, 4, 1), axis=0)
    return cover[0], gains


def solution(mesh):
    torus = Mesh(mesh.devices.reshape(SIZES), AXES)
    return jax.shard_map(
        local,
        mesh=torus,
        in_specs=(P(AXES, None), P(AXES), P(), P(BLK)),
        out_specs=(P(AXES), P(AXES)),
        check_vma=False,
    )
```

```python
import functools

import jax
import jax.numpy as jnp
from jax import lax
from jax.experimental import pallas as pl
from jax.experimental.pallas import tpu as pltpu
from jax.sharding import Mesh
from jax.sharding import PartitionSpec as P

AXES = ("ylo", "x", "yhi", "z", "core")
SIZES = (2, 4, 2, 8, 2)
BLK = ("ylo", "x")
CHIPS = ("ylo", "x", "yhi", "z")
MOST = 4
STEP = 512


def place(y, x, z, core):
    return (((y % 2) * 4 + x) * 2 + y // 2) * 16 + z * 2 + core


def pairs_of(move):
    return [
        (place(y, x, z, core), place(*move(y, x, z, core)))
        for y in range(4)
        for x in range(4)
        for z in range(8)
        for core in range(2)
    ]


def swap(value, y_mask, core_mask):
    return lax.ppermute(value, AXES, pairs_of(lambda y, x, z, c: (y ^ y_mask, x, z, c ^ core_mask)))


def turn(value, mask, first):
    return lax.ppermute(
        value,
        AXES,
        pairs_of(lambda y, x, z, c: (y, x ^ mask, z, c) if (c == 0) == first else (y ^ mask, x, z, c)),
    )


def turned_table(pieces, turned):
    for k, piece in enumerate(pieces):
        turned[:, k * 128 : k * 128 + 128] = piece[...].T


def tile_sims(table, turned, start):
    return jnp.dot(table[pl.ds(start, STEP), :], turned[...], preferred_element_type=jnp.float32)


def best_kernel(own_ref, floor_ref, c0, c1, partner_ref, best_ref, turned):
    rows, width = own_ref.shape
    scale = 1.0 / width**0.5
    turned_table((c0, c1), turned)
    for t, table in enumerate((own_ref, partner_ref)):
        for start in range(0, rows, STEP):
            sims = tile_sims(table, turned, start)
            top = functools.reduce(jnp.maximum, [sims[:, l : l + 128] for l in range(0, 256, 128)])
            for r in range(0, STEP, 128):
                here = pl.ds(start + r, 128)
                row = jnp.max(top[r : r + 128].T, axis=0, keepdims=True) * scale
                if t < floor_ref.shape[0]:
                    row = jnp.maximum(row, floor_ref[t : t + 1, here])
                best_ref[t : t + 1, here] = row


def gains_over(tables, floors, pieces, turned):
    rows, width = tables[0].shape
    turned_table(pieces, turned)
    total = jnp.zeros((8, 256), jnp.float32)
    for t, table in enumerate(tables):
        for start in range(0, rows, STEP):
            sims = tile_sims(table, turned, start)
            for r in range(0, STEP, 128):
                line = floors(t, pl.ds(start + r, 128))
                floor = jnp.broadcast_to(line * width**0.5, (128, 128)).T
                over = jnp.maximum(sims[r : r + 128] - jnp.concatenate([floor] * 2, axis=1), 0.0)
                total = total + jnp.sum(over.reshape(16, 8, 256), axis=0)
    return jnp.sum(total, axis=0, keepdims=True) / width**0.5


def near_gain_kernel(own_ref, best_ref, other_ref, c0, c1, partner_ref, sums_ref, cover_ref, turned):
    def floors(t, here):
        line = jnp.maximum(best_ref[t : t + 1, here], other_ref[1 - t : 2 - t, here])
        if t == 0:
            cover_ref[:, here] = line
        return line

    sums = gains_over((own_ref, partner_ref), floors, (c0, c1), turned)
    sums_ref[...] = jnp.broadcast_to(sums, (8, 256))


def far_gain_kernel(own_ref, best_ref, other_ref, sums_ref, c0, c1, partner_ref, gain_ref, turned):
    def floors(t, here):
        return jnp.maximum(best_ref[t : t + 1, here], other_ref[1 - t : 2 - t, here])

    far = gains_over((own_ref, partner_ref), floors, (c0, c1), turned)
    halves = (sums_ref[:1, :], far)
    first = lax.axis_index("core") == 0
    x = lax.axis_index("x")
    yhi, ylo = lax.axis_index("yhi"), lax.axis_index("ylo")
    for late in range(4):
        for early in range(4):
            x_mask = jnp.where(first, early, late)
            y_mask = jnp.where(first, late, early)
            at = ((ylo ^ (y_mask & 1)) * 4 + (x ^ x_mask)) * 2 + (yhi ^ (y_mask >> 1))
            lane = late % 2 * 128 + early * 32
            gain_ref[pl.ds(at * 8, 8), :] = jnp.broadcast_to(halves[late // 2][:, lane : lane + 32], (8, 32))


def on_chip(kernel, outs, scratch, pieces, *operands):
    vmem = pl.BlockSpec(memory_space=pltpu.VMEM)
    return pl.pallas_call(
        kernel,
        out_shape=[jax.ShapeDtypeStruct(out, jnp.float32) for out in outs],
        in_specs=[vmem] * len(operands),
        out_specs=[vmem] * len(outs),
        scratch_shapes=scratch,
        compiler_params=pltpu.CompilerParams(vmem_limit_bytes=16 << 20),
        cost_estimate=pl.CostEstimate(flops=4096 * 128 * 768 * 2 * pieces, bytes_accessed=8 << 20, transcendentals=0),
    )(*operands)


def spot_kernel(rows, index_ref, targets_ref):
    core, yhi = lax.axis_index("core"), lax.axis_index("yhi")
    base = lax.axis_index(AXES) * rows

    lane = lax.broadcasted_iota(jnp.int32, (8, 128), 1)
    quarter = lane >> 5
    source = ((yhi ^ (quarter & 1)) << 6) | ((lane & 28) << 1) | ((core ^ (quarter >> 1)) << 2) | (lane & 3)
    wanted = jnp.take_along_axis(jnp.broadcast_to(index_ref[4:5, :], (8, 128)), source, axis=1) - base
    wanted = jnp.broadcast_to(wanted[:1], (128, 128)).T

    left = index_ref[:4, :] - base
    left = jnp.where((left >= 0) & (left < rows), left, rows).astype(jnp.float32)
    row = lax.broadcasted_iota(jnp.int32, (8, 128), 0)
    spots = jnp.full((8, 128), -1, jnp.int32)
    for s in range(MOST):
        least = jnp.min(jnp.min(left, axis=0, keepdims=True), axis=1, keepdims=True)
        left = jnp.where(left == least, float(rows), left)
        spots = jnp.where(row == s, least.astype(jnp.int32), spots)

    targets_ref[:128, :] = wanted
    targets_ref[128:, :] = spots


def pick_kernel(targets_ref, table, kept_ref, given_ref, found_ref):
    rows, width = table.shape
    targets = targets_ref[...]
    step = 512
    lanes = lax.broadcasted_iota(jnp.int32, (136, 128), 1)
    total = jnp.zeros((136, width), jnp.float32)
    for k in range(rows // step):
        hits = [targets == lanes + (k * step + l) for l in range(0, step, 128)]
        pick = jnp.concatenate([jnp.where(h, 1.0, 0.0).astype(jnp.bfloat16) for h in hits], axis=1)
        total = total + jnp.dot(pick, table[pl.ds(k * step, step), :], preferred_element_type=jnp.float32)
    kept_ref[...] = total[:64].astype(jnp.bfloat16)
    given_ref[...] = total[64:128].astype(jnp.bfloat16)
    found_ref[...] = total[128 : 128 + MOST].astype(jnp.bfloat16)


def settle_kernel(got_ref, block_ref):
    total = got_ref[0, :32, :].astype(jnp.float32)
    for z in range(1, 8):
        total = total + got_ref[z, :32, :].astype(jnp.float32)
    block_ref[:32, :] = total.astype(jnp.bfloat16)
    found = [got_ref[z, 32:, :].astype(jnp.float32) for z in range(8)]
    block_ref[32:, :] = jnp.concatenate(found, axis=0).astype(jnp.bfloat16)


def settled(got):
    vmem = pl.BlockSpec(memory_space=pltpu.VMEM)
    return pl.pallas_call(
        settle_kernel,
        out_shape=jax.ShapeDtypeStruct((64, got.shape[2]), jnp.bfloat16),
        in_specs=[vmem],
        out_specs=vmem,
        compiler_params=pltpu.CompilerParams(vmem_limit_bytes=8 << 20),
        cost_estimate=pl.CostEstimate(flops=1 << 20, bytes_accessed=1 << 20, transcendentals=0),
    )(got)


def own_picks(chosen_index, candidate_index, embeddings):
    rows, width = embeddings.shape
    index = jnp.concatenate([chosen_index, candidate_index]).reshape(5, 128)
    vmem = pl.BlockSpec(memory_space=pltpu.VMEM)
    targets = pl.pallas_call(
        functools.partial(spot_kernel, rows),
        out_shape=jax.ShapeDtypeStruct((136, 128), jnp.int32),
        in_specs=[vmem],
        out_specs=vmem,
        compiler_params=pltpu.CompilerParams(vmem_limit_bytes=8 << 20),
        cost_estimate=pl.CostEstimate(flops=1 << 32, bytes_accessed=1 << 17, transcendentals=0),
    )(index)
    return pl.pallas_call(
        pick_kernel,
        out_shape=[jax.ShapeDtypeStruct((64, width), jnp.bfloat16)] * 2
        + [jax.ShapeDtypeStruct((MOST, width), jnp.bfloat16)],
        in_specs=[vmem] * 2,
        out_specs=[vmem] * 3,
        compiler_params=pltpu.CompilerParams(vmem_limit_bytes=40 << 20),
        cost_estimate=pl.CostEstimate(flops=136 * 2048 * 768 * 2, bytes_accessed=4 << 20, transcendentals=0),
    )(targets, embeddings)


def local(embeddings, coverage, chosen_index, candidate_index):
    rows, width = embeddings.shape
    kept, given, found = own_picks(chosen_index, candidate_index, embeddings)
    half = kept + swap(given, 0, 1)
    half, later = lax.optimization_barrier((half, embeddings))
    partner = swap(later, 0, 1)
    quarter = half[:32] + swap(half[32:], 2, 0)
    send = jnp.concatenate([quarter, found], axis=0)
    got = lax.all_to_all(jnp.broadcast_to(send, (8, 32 + MOST, width)), "z", 0, 0)
    block = settled(got)
    line = jnp.stack([block] + [turn(block, s, True) for s in (1, 2, 3)])
    cands, chosen = line[:, :32].reshape(128, width), line[:, 32:].reshape(128, width)
    chosen = [chosen] + [turn(chosen, s, False) for s in (1, 2, 3)]
    cands = [cands] + [turn(cands, s, False) for s in (1, 2, 3)]

    table = [pltpu.VMEM((width, 256), jnp.bfloat16)]
    best = coverage.reshape(1, rows)
    for pieces in (chosen[:2], chosen[2:]):
        best = on_chip(best_kernel, [(2, rows)], table, 2, embeddings, best, *pieces, partner)[0]
    other = swap(best, 0, 1)
    sums, cover = on_chip(
        near_gain_kernel, [(8, 256), (1, rows)], table, 2, embeddings, best, other, *cands[:2], partner
    )
    part = on_chip(far_gain_kernel, [(128, 32)], table, 2, embeddings, best, other, sums, *cands[2:], partner)[0]
    parts = lax.all_to_all(part, CHIPS, 0, 0, tiled=True)
    gains = jnp.sum(lax.dynamic_slice_in_dim(parts, lax.axis_index("z") * 4, 4, 1), axis=0)
    return cover[0], gains


def solution(mesh):
    torus = Mesh(mesh.devices.reshape(SIZES), AXES)
    return jax.shard_map(
        local,
        mesh=torus,
        in_specs=(P(AXES, None), P(AXES), P(), P(BLK)),
        out_specs=(P(AXES), P(AXES)),
        check_vma=False,
    )
```

```python
import functools

import jax
import jax.numpy as jnp
from jax import lax
from jax.experimental import pallas as pl
from jax.experimental.pallas import tpu as pltpu
from jax.sharding import Mesh
from jax.sharding import PartitionSpec as P

AXES = ("ylo", "x", "yhi", "z", "core")
SIZES = (2, 4, 2, 8, 2)
BLK = ("ylo", "x")
CHIPS = ("ylo", "x", "yhi", "z")
MOST = 4
STEP = 512


def place(y, x, z, core):
    return (((y % 2) * 4 + x) * 2 + y // 2) * 16 + z * 2 + core


def pairs_of(move):
    return [
        (place(y, x, z, core), place(*move(y, x, z, core)))
        for y in range(4)
        for x in range(4)
        for z in range(8)
        for core in range(2)
    ]


def swap(value, y_mask, core_mask):
    return lax.ppermute(value, AXES, pairs_of(lambda y, x, z, c: (y ^ y_mask, x, z, c ^ core_mask)))


def turn(value, mask, first):
    return lax.ppermute(
        value,
        AXES,
        pairs_of(lambda y, x, z, c: (y, x ^ mask, z, c) if (c == 1) == first else (y ^ mask, x, z, c)),
    )


def turned_table(pieces, turned):
    for k, piece in enumerate(pieces):
        turned[:, k * 128 : k * 128 + 128] = piece[...].T


def tile_sims(table, turned, start):
    return jnp.dot(table[pl.ds(start, STEP), :], turned[...], preferred_element_type=jnp.float32)


def turn_kernel(c0, c1, c2, c3, turned):
    turned_table((c0, c1, c2, c3), turned)


def turned_pieces(pieces):
    vmem = pl.BlockSpec(memory_space=pltpu.VMEM)
    return pl.pallas_call(
        turn_kernel,
        out_shape=jax.ShapeDtypeStruct((pieces[0].shape[1], 512), jnp.bfloat16),
        in_specs=[vmem] * 4,
        out_specs=vmem,
        compiler_params=pltpu.CompilerParams(vmem_limit_bytes=8 << 20),
        cost_estimate=pl.CostEstimate(flops=1 << 20, bytes_accessed=2 << 20, transcendentals=0),
    )(*pieces)


def best_kernel(own_ref, floor_ref, c0, c1, partner_ref, best_ref, turned):
    rows, width = own_ref.shape
    scale = 1.0 / width**0.5
    turned_table((c0, c1), turned)
    for t, table in enumerate((own_ref, partner_ref)):
        for start in range(0, rows, STEP):
            sims = tile_sims(table, turned, start)
            top = functools.reduce(jnp.maximum, [sims[:, l : l + 128] for l in range(0, 256, 128)])
            for r in range(0, STEP, 128):
                here = pl.ds(start + r, 128)
                row = jnp.max(top[r : r + 128].T, axis=0, keepdims=True) * scale
                if t < floor_ref.shape[0]:
                    row = jnp.maximum(row, floor_ref[t : t + 1, here])
                best_ref[t : t + 1, here] = row


def gain_kernel(own_ref, best_ref, other_ref, turned, partner_ref, gain_ref, cover_ref):
    rows, width = own_ref.shape
    scale = 1.0 / width**0.5
    total = jnp.zeros((8, 512), jnp.float32)
    for t, table in enumerate((own_ref, partner_ref)):
        for start in range(0, rows, STEP):
            sims = tile_sims(table, turned, start)
            for r in range(0, STEP, 128):
                here = pl.ds(start + r, 128)
                line = jnp.maximum(best_ref[t : t + 1, here], other_ref[1 - t : 2 - t, here])
                if t == 0:
                    cover_ref[:, here] = line
                floor = jnp.broadcast_to(line * width**0.5, (128, 128)).T
                over = jnp.maximum(sims[r : r + 128] - jnp.concatenate([floor] * 4, axis=1), 0.0)
                total = total + jnp.sum(over.reshape(16, 8, 512), axis=0)
    sums = jnp.sum(total, axis=0, keepdims=True) * scale
    first = lax.axis_index("core") == 1
    x = lax.axis_index("x")
    yhi, ylo = lax.axis_index("yhi"), lax.axis_index("ylo")
    for late in range(4):
        for early in range(4):
            x_mask = jnp.where(first, early, late)
            y_mask = jnp.where(first, late, early)
            at = ((ylo ^ (y_mask & 1)) * 4 + (x ^ x_mask)) * 2 + (yhi ^ (y_mask >> 1))
            lane = late * 128 + early * 32
            gain_ref[pl.ds(at * 8, 8), :] = jnp.broadcast_to(sums[:, lane : lane + 32], (8, 32))


def on_chip(kernel, outs, scratch, pieces, *operands):
    vmem = pl.BlockSpec(memory_space=pltpu.VMEM)
    return pl.pallas_call(
        kernel,
        out_shape=[jax.ShapeDtypeStruct(out, jnp.float32) for out in outs],
        in_specs=[vmem] * len(operands),
        out_specs=[vmem] * len(outs),
        scratch_shapes=scratch,
        compiler_params=pltpu.CompilerParams(vmem_limit_bytes=16 << 20),
        cost_estimate=pl.CostEstimate(flops=4096 * 128 * 768 * 2 * pieces, bytes_accessed=8 << 20, transcendentals=0),
    )(*operands)


def spot_kernel(rows, index_ref, targets_ref):
    core, yhi = lax.axis_index("core"), lax.axis_index("yhi")
    base = lax.axis_index(AXES) * rows

    lane = lax.broadcasted_iota(jnp.int32, (8, 128), 1)
    quarter = lane >> 5
    source = ((yhi ^ (quarter & 1)) << 6) | ((lane & 28) << 1) | ((core ^ (quarter >> 1)) << 2) | (lane & 3)
    wanted = jnp.take_along_axis(jnp.broadcast_to(index_ref[4:5, :], (8, 128)), source, axis=1) - base
    wanted = jnp.broadcast_to(wanted[:1], (128, 128)).T

    left = index_ref[:4, :] - base
    left = jnp.where((left >= 0) & (left < rows), left, rows).astype(jnp.float32)
    row = lax.broadcasted_iota(jnp.int32, (8, 128), 0)
    spots = jnp.full((8, 128), -1, jnp.int32)
    for s in range(MOST):
        least = jnp.min(jnp.min(left, axis=0, keepdims=True), axis=1, keepdims=True)
        left = jnp.where(left == least, float(rows), left)
        spots = jnp.where(row == s, least.astype(jnp.int32), spots)

    targets_ref[:128, :] = wanted
    targets_ref[128:, :] = spots


def pick_kernel(targets_ref, table, kept_ref, given_ref, found_ref):
    rows, width = table.shape
    targets = targets_ref[...]
    step = 512
    lanes = lax.broadcasted_iota(jnp.int32, (136, 128), 1)
    total = jnp.zeros((136, width), jnp.float32)
    for k in range(rows // step):
        hits = [targets == lanes + (k * step + l) for l in range(0, step, 128)]
        pick = jnp.concatenate([jnp.where(h, 1.0, 0.0).astype(jnp.bfloat16) for h in hits], axis=1)
        total = total + jnp.dot(pick, table[pl.ds(k * step, step), :], preferred_element_type=jnp.float32)
    kept_ref[...] = total[:64].astype(jnp.bfloat16)
    given_ref[...] = total[64:128].astype(jnp.bfloat16)
    found_ref[...] = total[128 : 128 + MOST].astype(jnp.bfloat16)


def settle_kernel(got_ref, block_ref):
    total = got_ref[0, :32, :].astype(jnp.float32)
    for z in range(1, 8):
        total = total + got_ref[z, :32, :].astype(jnp.float32)
    block_ref[:32, :] = total.astype(jnp.bfloat16)
    found = [got_ref[z, 32:, :].astype(jnp.float32) for z in range(8)]
    block_ref[32:, :] = jnp.concatenate(found, axis=0).astype(jnp.bfloat16)


def settled(got):
    vmem = pl.BlockSpec(memory_space=pltpu.VMEM)
    return pl.pallas_call(
        settle_kernel,
        out_shape=jax.ShapeDtypeStruct((64, got.shape[2]), jnp.bfloat16),
        in_specs=[vmem],
        out_specs=vmem,
        compiler_params=pltpu.CompilerParams(vmem_limit_bytes=8 << 20),
        cost_estimate=pl.CostEstimate(flops=1 << 20, bytes_accessed=1 << 20, transcendentals=0),
    )(got)


def own_picks(chosen_index, candidate_index, embeddings):
    rows, width = embeddings.shape
    index = jnp.concatenate([chosen_index, candidate_index]).reshape(5, 128)
    vmem = pl.BlockSpec(memory_space=pltpu.VMEM)
    targets = pl.pallas_call(
        functools.partial(spot_kernel, rows),
        out_shape=jax.ShapeDtypeStruct((136, 128), jnp.int32),
        in_specs=[vmem],
        out_specs=vmem,
        compiler_params=pltpu.CompilerParams(vmem_limit_bytes=8 << 20),
        cost_estimate=pl.CostEstimate(flops=1 << 32, bytes_accessed=1 << 17, transcendentals=0),
    )(index)
    return pl.pallas_call(
        pick_kernel,
        out_shape=[jax.ShapeDtypeStruct((64, width), jnp.bfloat16)] * 2
        + [jax.ShapeDtypeStruct((MOST, width), jnp.bfloat16)],
        in_specs=[vmem] * 2,
        out_specs=[vmem] * 3,
        compiler_params=pltpu.CompilerParams(vmem_limit_bytes=40 << 20),
        cost_estimate=pl.CostEstimate(flops=136 * 2048 * 768 * 2, bytes_accessed=4 << 20, transcendentals=0),
    )(targets, embeddings)


def local(embeddings, coverage, chosen_index, candidate_index):
    rows, width = embeddings.shape
    kept, given, found = own_picks(chosen_index, candidate_index, embeddings)
    half = kept + swap(given, 0, 1)
    half, later = lax.optimization_barrier((half, embeddings))
    partner = swap(later, 0, 1)
    quarter = half[:32] + swap(half[32:], 2, 0)
    send = jnp.concatenate([quarter, found], axis=0)
    got = lax.all_to_all(jnp.broadcast_to(send, (8, 32 + MOST, width)), "z", 0, 0)
    block = settled(got)
    line = jnp.stack([block] + [turn(block, s, True) for s in (1, 2, 3)])
    cands, chosen = line[:, :32].reshape(128, width), line[:, 32:].reshape(128, width)
    chosen = [chosen] + [turn(chosen, s, False) for s in (1, 2, 3)]
    cands = [cands] + [turn(cands, s, False) for s in (1, 2, 3)]

    table = [pltpu.VMEM((width, 256), jnp.bfloat16)]
    best = coverage.reshape(1, rows)
    for pieces in (chosen[:2], chosen[2:]):
        best = on_chip(best_kernel, [(2, rows)], table, 2, embeddings, best, *pieces, partner)[0]
    other = swap(best, 0, 1)
    turned = turned_pieces(cands)
    part, cover = on_chip(gain_kernel, [(128, 32), (1, rows)], [], 4, embeddings, best, other, turned, partner)
    parts = lax.all_to_all(part, CHIPS, 0, 0, tiled=True)
    gains = jnp.sum(lax.dynamic_slice_in_dim(parts, lax.axis_index("z") * 4, 4, 1), axis=0)
    return cover[0], gains


def solution(mesh):
    torus = Mesh(mesh.devices.reshape(SIZES), AXES)
    return jax.shard_map(
        local,
        mesh=torus,
        in_specs=(P(AXES, None), P(AXES), P(), P(BLK)),
        out_specs=(P(AXES), P(AXES)),
        check_vma=False,
    )
```

```python
import functools

import jax
import jax.numpy as jnp
from jax import lax
from jax.experimental import pallas as pl
from jax.experimental.pallas import tpu as pltpu
from jax.sharding import Mesh
from jax.sharding import PartitionSpec as P

AXES = ("ylo", "x", "yhi", "z", "core")
SIZES = (2, 4, 2, 8, 2)
BLK = ("ylo", "x")
CHIPS = ("ylo", "x", "yhi", "z")
MOST = 4
STEP = 512


def place(y, x, z, core):
    return (((y % 2) * 4 + x) * 2 + y // 2) * 16 + z * 2 + core


def pairs_of(move):
    return [
        (place(y, x, z, core), place(*move(y, x, z, core)))
        for y in range(4)
        for x in range(4)
        for z in range(8)
        for core in range(2)
    ]


def swap(value, y_mask, core_mask):
    return lax.ppermute(value, AXES, pairs_of(lambda y, x, z, c: (y ^ y_mask, x, z, c ^ core_mask)))


def turn(value, mask, first):
    return lax.ppermute(
        value,
        AXES,
        pairs_of(lambda y, x, z, c: (y, x ^ mask, z, c) if (c == 0) == first else (y ^ mask, x, z, c)),
    )


def ring_of(piece):
    near, back = turn(piece, 1, False), turn(piece, 3, False)
    across = [turn(back[:64], 1, False), turn(near[64:], 3, False)]
    return [piece, near, jnp.concatenate(across), back]


def turned_table(pieces, turned):
    for k, piece in enumerate(pieces):
        turned[:, k * 128 : k * 128 + 128] = piece[...].T


def tile_sims(table, turned, start):
    return jnp.dot(table[pl.ds(start, STEP), :], turned[...], preferred_element_type=jnp.float32)


def turn_kernel(c0, c1, c2, c3, turned):
    turned_table((c0, c1, c2, c3), turned)


def turned_pieces(pieces):
    vmem = pl.BlockSpec(memory_space=pltpu.VMEM)
    return pl.pallas_call(
        turn_kernel,
        out_shape=jax.ShapeDtypeStruct((pieces[0].shape[1], 512), jnp.bfloat16),
        in_specs=[vmem] * 4,
        out_specs=vmem,
        compiler_params=pltpu.CompilerParams(vmem_limit_bytes=8 << 20),
        cost_estimate=pl.CostEstimate(flops=1 << 20, bytes_accessed=2 << 20, transcendentals=0),
    )(*pieces)


def best_kernel(own_ref, floor_ref, c0, c1, partner_ref, best_ref, turned):
    rows, width = own_ref.shape
    scale = 1.0 / width**0.5
    turned_table((c0, c1), turned)
    for t, table in enumerate((own_ref, partner_ref)):
        for start in range(0, rows, STEP):
            sims = tile_sims(table, turned, start)
            top = functools.reduce(jnp.maximum, [sims[:, l : l + 128] for l in range(0, 256, 128)])
            for r in range(0, STEP, 128):
                here = pl.ds(start + r, 128)
                row = jnp.max(top[r : r + 128].T, axis=0, keepdims=True) * scale
                if t < floor_ref.shape[0]:
                    row = jnp.maximum(row, floor_ref[t : t + 1, here])
                best_ref[t : t + 1, here] = row


def gain_kernel(own_ref, best_ref, other_ref, turned, partner_ref, gain_ref, cover_ref):
    rows, width = own_ref.shape
    scale = 1.0 / width**0.5
    total = jnp.zeros((8, 512), jnp.float32)
    for t, table in enumerate((own_ref, partner_ref)):
        for start in range(0, rows, STEP):
            sims = tile_sims(table, turned, start)
            for r in range(0, STEP, 128):
                here = pl.ds(start + r, 128)
                line = jnp.maximum(best_ref[t : t + 1, here], other_ref[1 - t : 2 - t, here])
                if t == 0:
                    cover_ref[:, here] = line
                floor = jnp.broadcast_to(line * width**0.5, (128, 128)).T
                over = jnp.maximum(sims[r : r + 128] - jnp.concatenate([floor] * 4, axis=1), 0.0)
                total = total + jnp.sum(over.reshape(16, 8, 512), axis=0)
    sums = jnp.sum(total, axis=0, keepdims=True) * scale
    first = lax.axis_index("core") == 0
    x = lax.axis_index("x")
    yhi, ylo = lax.axis_index("yhi"), lax.axis_index("ylo")
    for late in range(4):
        for early in range(4):
            x_mask = jnp.where(first, early, late)
            y_mask = jnp.where(first, late, early)
            at = ((ylo ^ (y_mask & 1)) * 4 + (x ^ x_mask)) * 2 + (yhi ^ (y_mask >> 1))
            lane = late * 128 + early * 32
            gain_ref[pl.ds(at * 8, 8), :] = jnp.broadcast_to(sums[:, lane : lane + 32], (8, 32))


def on_chip(kernel, outs, scratch, pieces, *operands):
    vmem = pl.BlockSpec(memory_space=pltpu.VMEM)
    return pl.pallas_call(
        kernel,
        out_shape=[jax.ShapeDtypeStruct(out, jnp.float32) for out in outs],
        in_specs=[vmem] * len(operands),
        out_specs=[vmem] * len(outs),
        scratch_shapes=scratch,
        compiler_params=pltpu.CompilerParams(vmem_limit_bytes=16 << 20),
        cost_estimate=pl.CostEstimate(flops=4096 * 128 * 768 * 2 * pieces, bytes_accessed=8 << 20, transcendentals=0),
    )(*operands)


def spot_kernel(rows, index_ref, targets_ref):
    core, yhi = lax.axis_index("core"), lax.axis_index("yhi")
    base = lax.axis_index(AXES) * rows

    lane = lax.broadcasted_iota(jnp.int32, (8, 128), 1)
    quarter = lane >> 5
    source = ((yhi ^ (quarter & 1)) << 6) | ((lane & 28) << 1) | ((core ^ (quarter >> 1)) << 2) | (lane & 3)
    wanted = jnp.take_along_axis(jnp.broadcast_to(index_ref[4:5, :], (8, 128)), source, axis=1) - base
    wanted = jnp.broadcast_to(wanted[:1], (128, 128)).T

    left = index_ref[:4, :] - base
    left = jnp.where((left >= 0) & (left < rows), left, rows).astype(jnp.float32)
    row = lax.broadcasted_iota(jnp.int32, (8, 128), 0)
    spots = jnp.full((8, 128), -1, jnp.int32)
    for s in range(MOST):
        least = jnp.min(jnp.min(left, axis=0, keepdims=True), axis=1, keepdims=True)
        left = jnp.where(left == least, float(rows), left)
        spots = jnp.where(row == s, least.astype(jnp.int32), spots)

    targets_ref[:128, :] = wanted
    targets_ref[128:, :] = spots


def pick_kernel(targets_ref, table, kept_ref, given_ref, found_ref):
    rows, width = table.shape
    targets = targets_ref[...]
    step = 512
    lanes = lax.broadcasted_iota(jnp.int32, (136, 128), 1)
    total = jnp.zeros((136, width), jnp.float32)
    for k in range(rows // step):
        hits = [targets == lanes + (k * step + l) for l in range(0, step, 128)]
        pick = jnp.concatenate([jnp.where(h, 1.0, 0.0).astype(jnp.bfloat16) for h in hits], axis=1)
        total = total + jnp.dot(pick, table[pl.ds(k * step, step), :], preferred_element_type=jnp.float32)
    kept_ref[...] = total[:64].astype(jnp.bfloat16)
    given_ref[...] = total[64:128].astype(jnp.bfloat16)
    found_ref[...] = total[128 : 128 + MOST].astype(jnp.bfloat16)


def settle_kernel(got_ref, block_ref):
    total = got_ref[0, :32, :].astype(jnp.float32)
    for z in range(1, 8):
        total = total + got_ref[z, :32, :].astype(jnp.float32)
    block_ref[:32, :] = total.astype(jnp.bfloat16)
    found = [got_ref[z, 32:, :].astype(jnp.float32) for z in range(8)]
    block_ref[32:, :] = jnp.concatenate(found, axis=0).astype(jnp.bfloat16)


def settled(got):
    vmem = pl.BlockSpec(memory_space=pltpu.VMEM)
    return pl.pallas_call(
        settle_kernel,
        out_shape=jax.ShapeDtypeStruct((64, got.shape[2]), jnp.bfloat16),
        in_specs=[vmem],
        out_specs=vmem,
        compiler_params=pltpu.CompilerParams(vmem_limit_bytes=8 << 20),
        cost_estimate=pl.CostEstimate(flops=1 << 20, bytes_accessed=1 << 20, transcendentals=0),
    )(got)


def own_picks(chosen_index, candidate_index, embeddings):
    rows, width = embeddings.shape
    index = jnp.concatenate([chosen_index, candidate_index]).reshape(5, 128)
    vmem = pl.BlockSpec(memory_space=pltpu.VMEM)
    targets = pl.pallas_call(
        functools.partial(spot_kernel, rows),
        out_shape=jax.ShapeDtypeStruct((136, 128), jnp.int32),
        in_specs=[vmem],
        out_specs=vmem,
        compiler_params=pltpu.CompilerParams(vmem_limit_bytes=8 << 20),
        cost_estimate=pl.CostEstimate(flops=1 << 32, bytes_accessed=1 << 17, transcendentals=0),
    )(index)
    return pl.pallas_call(
        pick_kernel,
        out_shape=[jax.ShapeDtypeStruct((64, width), jnp.bfloat16)] * 2
        + [jax.ShapeDtypeStruct((MOST, width), jnp.bfloat16)],
        in_specs=[vmem] * 2,
        out_specs=[vmem] * 3,
        compiler_params=pltpu.CompilerParams(vmem_limit_bytes=40 << 20),
        cost_estimate=pl.CostEstimate(flops=136 * 2048 * 768 * 2, bytes_accessed=4 << 20, transcendentals=0),
    )(targets, embeddings)


def local(embeddings, coverage, chosen_index, candidate_index):
    rows, width = embeddings.shape
    kept, given, found = own_picks(chosen_index, candidate_index, embeddings)
    half = kept + swap(given, 0, 1)
    half, later = lax.optimization_barrier((half, embeddings))
    partner = swap(later, 0, 1)
    quarter = half[:32] + swap(half[32:], 2, 0)
    send = jnp.concatenate([quarter, found], axis=0)
    got = lax.all_to_all(jnp.broadcast_to(send, (8, 32 + MOST, width)), "z", 0, 0)
    block = settled(got)
    line = jnp.stack([block] + [turn(block, s, True) for s in (1, 2, 3)])
    cands, chosen = line[:, :32].reshape(128, width), line[:, 32:].reshape(128, width)
    chosen, cands = ring_of(chosen), ring_of(cands)

    table = [pltpu.VMEM((width, 256), jnp.bfloat16)]
    best = coverage.reshape(1, rows)
    for pieces in (chosen[:2], chosen[2:]):
        best = on_chip(best_kernel, [(2, rows)], table, 2, embeddings, best, *pieces, partner)[0]
    other = swap(best, 0, 1)
    turned = turned_pieces(cands)
    part, cover = on_chip(gain_kernel, [(128, 32), (1, rows)], [], 4, embeddings, best, other, turned, partner)
    parts = lax.all_to_all(part, CHIPS, 0, 0, tiled=True)
    gains = jnp.sum(lax.dynamic_slice_in_dim(parts, lax.axis_index("z") * 4, 4, 1), axis=0)
    return cover[0], gains


def solution(mesh):
    torus = Mesh(mesh.devices.reshape(SIZES), AXES)
    return jax.shard_map(
        local,
        mesh=torus,
        in_specs=(P(AXES, None), P(AXES), P(), P(BLK)),
        out_specs=(P(AXES), P(AXES)),
        check_vma=False,
    )
```

```python
import functools

import jax
import jax.numpy as jnp
from jax import lax
from jax.experimental import pallas as pl
from jax.experimental.pallas import tpu as pltpu
from jax.sharding import Mesh
from jax.sharding import PartitionSpec as P

AXES = ("ylo", "x", "yhi", "z", "core")
SIZES = (2, 4, 2, 8, 2)
BLK = ("ylo", "x")
CHIPS = ("ylo", "x", "yhi", "z")
MOST = 4
STEP = 512


def place(y, x, z, core):
    return (((y % 2) * 4 + x) * 2 + y // 2) * 16 + z * 2 + core


def pairs_of(move):
    return [
        (place(y, x, z, core), place(*move(y, x, z, core)))
        for y in range(4)
        for x in range(4)
        for z in range(8)
        for core in range(2)
    ]


def swap(value, y_mask, core_mask):
    return lax.ppermute(value, AXES, pairs_of(lambda y, x, z, c: (y ^ y_mask, x, z, c ^ core_mask)))


def turn(value, mask, first):
    return lax.ppermute(
        value,
        AXES,
        pairs_of(lambda y, x, z, c: (y, x ^ mask, z, c) if (c == 0) == first else (y ^ mask, x, z, c)),
    )


def turned_table(pieces, turned):
    for k, piece in enumerate(pieces):
        turned[:, k * 128 : k * 128 + 128] = piece[...].T


def tile_sims(table, turned, start):
    return jnp.dot(table[pl.ds(start, STEP), :], turned[...], preferred_element_type=jnp.float32)


def best_kernel(own_ref, floor_ref, c0, c1, partner_ref, best_ref, turned):
    rows, width = own_ref.shape
    scale = 1.0 / width**0.5
    turned_table((c0, c1), turned)
    for t, table in enumerate((own_ref, partner_ref)):
        for start in range(0, rows, STEP):
            sims = tile_sims(table, turned, start)
            top = functools.reduce(jnp.maximum, [sims[:, l : l + 128] for l in range(0, 256, 128)])
            for r in range(0, STEP, 128):
                here = pl.ds(start + r, 128)
                row = jnp.max(top[r : r + 128].T, axis=0, keepdims=True) * scale
                if t < floor_ref.shape[0]:
                    row = jnp.maximum(row, floor_ref[t : t + 1, here])
                best_ref[t : t + 1, here] = row


def gains_over(tables, floors, pieces, turned):
    rows, width = tables[0].shape
    turned_table(pieces, turned)
    total = jnp.zeros((8, 256), jnp.float32)
    for t, table in enumerate(tables):
        for start in range(0, rows, STEP):
            sims = tile_sims(table, turned, start)
            for r in range(0, STEP, 128):
                floor = floors(t, start + r)
                over = jnp.maximum(sims[r : r + 128] - jnp.concatenate([floor] * 2, axis=1), 0.0)
                total = total + jnp.sum(over.reshape(16, 8, 256), axis=0)
    return jnp.sum(total, axis=0, keepdims=True) / width**0.5


def near_gain_kernel(own_ref, best_ref, other_ref, c0, c1, partner_ref, sums_ref, cover_ref, floor_ref, turned):
    rows, width = own_ref.shape

    def floors(t, start):
        here = pl.ds(start, 128)
        line = jnp.maximum(best_ref[t : t + 1, here], other_ref[1 - t : 2 - t, here])
        if t == 0:
            cover_ref[:, here] = line
        floor = jnp.broadcast_to(line * width**0.5, (128, 128)).T
        floor_ref[pl.ds(t * rows + start, 128), :] = floor
        return floor

    sums = gains_over((own_ref, partner_ref), floors, (c0, c1), turned)
    sums_ref[...] = jnp.broadcast_to(sums, (8, 256))


def far_gain_kernel(own_ref, floor_ref, sums_ref, c0, c1, partner_ref, gain_ref, turned):
    rows = own_ref.shape[0]

    def floors(t, start):
        return floor_ref[pl.ds(t * rows + start, 128), :]

    far = gains_over((own_ref, partner_ref), floors, (c0, c1), turned)
    halves = (sums_ref[:1, :], far)
    first = lax.axis_index("core") == 0
    x = lax.axis_index("x")
    yhi, ylo = lax.axis_index("yhi"), lax.axis_index("ylo")
    for late in range(4):
        for early in range(4):
            x_mask = jnp.where(first, early, late)
            y_mask = jnp.where(first, late, early)
            at = ((ylo ^ (y_mask & 1)) * 4 + (x ^ x_mask)) * 2 + (yhi ^ (y_mask >> 1))
            lane = late % 2 * 128 + early * 32
            gain_ref[pl.ds(at * 8, 8), :] = jnp.broadcast_to(halves[late // 2][:, lane : lane + 32], (8, 32))


def on_chip(kernel, outs, scratch, pieces, *operands):
    vmem = pl.BlockSpec(memory_space=pltpu.VMEM)
    return pl.pallas_call(
        kernel,
        out_shape=[jax.ShapeDtypeStruct(out, jnp.float32) for out in outs],
        in_specs=[vmem] * len(operands),
        out_specs=[vmem] * len(outs),
        scratch_shapes=scratch,
        compiler_params=pltpu.CompilerParams(vmem_limit_bytes=16 << 20),
        cost_estimate=pl.CostEstimate(flops=4096 * 128 * 768 * 2 * pieces, bytes_accessed=8 << 20, transcendentals=0),
    )(*operands)


def spot_kernel(rows, index_ref, targets_ref):
    core, yhi = lax.axis_index("core"), lax.axis_index("yhi")
    base = lax.axis_index(AXES) * rows

    lane = lax.broadcasted_iota(jnp.int32, (8, 128), 1)
    quarter = lane >> 5
    source = ((yhi ^ (quarter & 1)) << 6) | ((lane & 28) << 1) | ((core ^ (quarter >> 1)) << 2) | (lane & 3)
    wanted = jnp.take_along_axis(jnp.broadcast_to(index_ref[4:5, :], (8, 128)), source, axis=1) - base
    wanted = jnp.broadcast_to(wanted[:1], (128, 128)).T

    left = index_ref[:4, :] - base
    left = jnp.where((left >= 0) & (left < rows), left, rows).astype(jnp.float32)
    row = lax.broadcasted_iota(jnp.int32, (8, 128), 0)
    spots = jnp.full((8, 128), -1, jnp.int32)
    for s in range(MOST):
        least = jnp.min(jnp.min(left, axis=0, keepdims=True), axis=1, keepdims=True)
        left = jnp.where(left == least, float(rows), left)
        spots = jnp.where(row == s, least.astype(jnp.int32), spots)

    targets_ref[:128, :] = wanted
    targets_ref[128:, :] = spots


def pick_kernel(targets_ref, table, kept_ref, given_ref, found_ref):
    rows, width = table.shape
    targets = targets_ref[...]
    step = 512
    lanes = lax.broadcasted_iota(jnp.int32, (136, 128), 1)
    total = jnp.zeros((136, width), jnp.float32)
    for k in range(rows // step):
        hits = [targets == lanes + (k * step + l) for l in range(0, step, 128)]
        pick = jnp.concatenate([jnp.where(h, 1.0, 0.0).astype(jnp.bfloat16) for h in hits], axis=1)
        total = total + jnp.dot(pick, table[pl.ds(k * step, step), :], preferred_element_type=jnp.float32)
    kept_ref[...] = total[:64].astype(jnp.bfloat16)
    given_ref[...] = total[64:128].astype(jnp.bfloat16)
    found_ref[...] = total[128 : 128 + MOST].astype(jnp.bfloat16)


def settle_kernel(got_ref, block_ref):
    total = got_ref[0, :32, :].astype(jnp.float32)
    for z in range(1, 8):
        total = total + got_ref[z, :32, :].astype(jnp.float32)
    block_ref[:32, :] = total.astype(jnp.bfloat16)
    found = [got_ref[z, 32:, :].astype(jnp.float32) for z in range(8)]
    block_ref[32:, :] = jnp.concatenate(found, axis=0).astype(jnp.bfloat16)


def settled(got):
    vmem = pl.BlockSpec(memory_space=pltpu.VMEM)
    return pl.pallas_call(
        settle_kernel,
        out_shape=jax.ShapeDtypeStruct((64, got.shape[2]), jnp.bfloat16),
        in_specs=[vmem],
        out_specs=vmem,
        compiler_params=pltpu.CompilerParams(vmem_limit_bytes=8 << 20),
        cost_estimate=pl.CostEstimate(flops=1 << 20, bytes_accessed=1 << 20, transcendentals=0),
    )(got)


def own_picks(chosen_index, candidate_index, embeddings):
    rows, width = embeddings.shape
    index = jnp.concatenate([chosen_index, candidate_index]).reshape(5, 128)
    vmem = pl.BlockSpec(memory_space=pltpu.VMEM)
    targets = pl.pallas_call(
        functools.partial(spot_kernel, rows),
        out_shape=jax.ShapeDtypeStruct((136, 128), jnp.int32),
        in_specs=[vmem],
        out_specs=vmem,
        compiler_params=pltpu.CompilerParams(vmem_limit_bytes=8 << 20),
        cost_estimate=pl.CostEstimate(flops=1 << 32, bytes_accessed=1 << 17, transcendentals=0),
    )(index)
    return pl.pallas_call(
        pick_kernel,
        out_shape=[jax.ShapeDtypeStruct((64, width), jnp.bfloat16)] * 2
        + [jax.ShapeDtypeStruct((MOST, width), jnp.bfloat16)],
        in_specs=[vmem] * 2,
        out_specs=[vmem] * 3,
        compiler_params=pltpu.CompilerParams(vmem_limit_bytes=40 << 20),
        cost_estimate=pl.CostEstimate(flops=136 * 2048 * 768 * 2, bytes_accessed=4 << 20, transcendentals=0),
    )(targets, embeddings)


def local(embeddings, coverage, chosen_index, candidate_index):
    rows, width = embeddings.shape
    kept, given, found = own_picks(chosen_index, candidate_index, embeddings)
    half = kept + swap(given, 0, 1)
    half, later = lax.optimization_barrier((half, embeddings))
    partner = swap(later, 0, 1)
    quarter = half[:32] + swap(half[32:], 2, 0)
    send = jnp.concatenate([quarter, found], axis=0)
    got = lax.all_to_all(jnp.broadcast_to(send, (8, 32 + MOST, width)), "z", 0, 0)
    block = settled(got)
    line = jnp.stack([block] + [turn(block, s, True) for s in (1, 2, 3)])
    cands, chosen = line[:, :32].reshape(128, width), line[:, 32:].reshape(128, width)
    chosen = [chosen] + [turn(chosen, s, False) for s in (1, 2, 3)]
    cands = [cands] + [turn(cands, s, False) for s in (1, 2, 3)]

    table = [pltpu.VMEM((width, 256), jnp.bfloat16)]
    best = coverage.reshape(1, rows)
    for pieces in (chosen[:2], chosen[2:]):
        best = on_chip(best_kernel, [(2, rows)], table, 2, embeddings, best, *pieces, partner)[0]
    other = swap(best, 0, 1)
    sums, cover, floor = on_chip(
        near_gain_kernel, [(8, 256), (1, rows), (2 * rows, 128)], table, 2, embeddings, best, other, *cands[:2], partner
    )
    part = on_chip(far_gain_kernel, [(128, 32)], table, 2, embeddings, floor, sums, *cands[2:], partner)[0]
    parts = lax.all_to_all(part, CHIPS, 0, 0, tiled=True)
    gains = jnp.sum(lax.dynamic_slice_in_dim(parts, lax.axis_index("z") * 4, 4, 1), axis=0)
    return cover[0], gains


def solution(mesh):
    torus = Mesh(mesh.devices.reshape(SIZES), AXES)
    return jax.shard_map(
        local,
        mesh=torus,
        in_specs=(P(AXES, None), P(AXES), P(), P(BLK)),
        out_specs=(P(AXES), P(AXES)),
        check_vma=False,
    )
```

```python
import functools

import jax
import jax.numpy as jnp
from jax import lax
from jax.experimental import pallas as pl
from jax.experimental.pallas import tpu as pltpu
from jax.sharding import Mesh
from jax.sharding import PartitionSpec as P

AXES = ("ylo", "x", "yhi", "z", "core")
SIZES = (2, 4, 2, 8, 2)
BLK = ("ylo", "x")
CHIPS = ("ylo", "x", "yhi", "z")
MOST = 4
STEP = 512


def place(y, x, z, core):
    return (((y % 2) * 4 + x) * 2 + y // 2) * 16 + z * 2 + core


def pairs_of(move):
    return [
        (place(y, x, z, core), place(*move(y, x, z, core)))
        for y in range(4)
        for x in range(4)
        for z in range(8)
        for core in range(2)
    ]


def swap(value, y_mask, core_mask):
    return lax.ppermute(value, AXES, pairs_of(lambda y, x, z, c: (y ^ y_mask, x, z, c ^ core_mask)))


def turn(value, mask, first):
    return lax.ppermute(
        value,
        AXES,
        pairs_of(lambda y, x, z, c: (y, x ^ mask, z, c) if (c == 0) == first else (y ^ mask, x, z, c)),
    )


def turned_table(pieces, turned):
    for k, piece in enumerate(pieces):
        turned[:, k * 128 : k * 128 + 128] = piece[...].T


def tile_sims(table, turned, start):
    return jnp.dot(table[pl.ds(start, STEP), :], turned[...], preferred_element_type=jnp.float32)


def turn_kernel(c0, c1, c2, c3, turned):
    turned_table((c0, c1, c2, c3), turned)


def turned_pieces(pieces):
    vmem = pl.BlockSpec(memory_space=pltpu.VMEM)
    return pl.pallas_call(
        turn_kernel,
        out_shape=jax.ShapeDtypeStruct((pieces[0].shape[1], 512), jnp.bfloat16),
        in_specs=[vmem] * 4,
        out_specs=vmem,
        compiler_params=pltpu.CompilerParams(vmem_limit_bytes=8 << 20),
        cost_estimate=pl.CostEstimate(flops=1 << 20, bytes_accessed=2 << 20, transcendentals=0),
    )(*pieces)


def best_kernel(own_ref, floor_ref, c0, c1, partner_ref, best_ref, turned):
    rows, width = own_ref.shape
    scale = 1.0 / width**0.5
    turned_table((c0, c1), turned)
    for t, table in enumerate((own_ref, partner_ref)):
        for start in range(0, rows, STEP):
            sims = tile_sims(table, turned, start)
            top = functools.reduce(jnp.maximum, [sims[:, l : l + 128] for l in range(0, 256, 128)])
            for r in range(0, STEP, 128):
                here = pl.ds(start + r, 128)
                row = jnp.max(top[r : r + 128].T, axis=0, keepdims=True) * scale
                if t < floor_ref.shape[0]:
                    row = jnp.maximum(row, floor_ref[t : t + 1, here])
                best_ref[t : t + 1, here] = row


def gain_kernel(own_ref, best_ref, other_ref, turned, partner_ref, gain_ref, cover_ref):
    rows, width = own_ref.shape
    scale = 1.0 / width**0.5
    total = jnp.zeros((8, 512), jnp.float32)
    for t, table in enumerate((own_ref, partner_ref)):
        for start in range(0, rows, STEP):
            sims = tile_sims(table, turned, start)
            for r in range(0, STEP, 128):
                here = pl.ds(start + r, 128)
                line = jnp.maximum(best_ref[t : t + 1, here], other_ref[1 - t : 2 - t, here])
                if t == 0:
                    cover_ref[:, here] = line
                floor = jnp.broadcast_to(line * width**0.5, (128, 128)).T
                over = jnp.maximum(sims[r : r + 128] - jnp.concatenate([floor] * 4, axis=1), 0.0)
                total = total + jnp.sum(over.reshape(16, 8, 512), axis=0)
    sums = jnp.sum(total, axis=0, keepdims=True) * scale
    first = lax.axis_index("core") == 0
    x = lax.axis_index("x")
    yhi, ylo = lax.axis_index("yhi"), lax.axis_index("ylo")
    for late in range(4):
        for early in range(4):
            x_mask = jnp.where(first, early, late)
            y_mask = jnp.where(first, late, early)
            at = ((ylo ^ (y_mask & 1)) * 4 + (x ^ x_mask)) * 2 + (yhi ^ (y_mask >> 1))
            lane = late * 128 + early * 32
            gain_ref[pl.ds(at * 8, 8), :] = jnp.broadcast_to(sums[:, lane : lane + 32], (8, 32))


def on_chip(kernel, outs, scratch, pieces, *operands):
    vmem = pl.BlockSpec(memory_space=pltpu.VMEM)
    return pl.pallas_call(
        kernel,
        out_shape=[jax.ShapeDtypeStruct(out, jnp.float32) for out in outs],
        in_specs=[vmem] * len(operands),
        out_specs=[vmem] * len(outs),
        scratch_shapes=scratch,
        compiler_params=pltpu.CompilerParams(vmem_limit_bytes=16 << 20),
        cost_estimate=pl.CostEstimate(flops=4096 * 128 * 768 * 2 * pieces, bytes_accessed=8 << 20, transcendentals=0),
    )(*operands)


def spot_kernel(rows, index_ref, targets_ref):
    core, yhi = lax.axis_index("core"), lax.axis_index("yhi")
    base = lax.axis_index(AXES) * rows

    lane = lax.broadcasted_iota(jnp.int32, (8, 128), 1)
    quarter = lane >> 5
    source = ((yhi ^ (quarter & 1)) << 6) | ((lane & 28) << 1) | ((core ^ (quarter >> 1)) << 2) | (lane & 3)
    wanted = jnp.take_along_axis(jnp.broadcast_to(index_ref[4:5, :], (8, 128)), source, axis=1) - base
    wanted = jnp.broadcast_to(wanted[:1], (128, 128)).T

    left = index_ref[:4, :] - base
    left = jnp.where((left >= 0) & (left < rows), left, rows).astype(jnp.float32)
    row = lax.broadcasted_iota(jnp.int32, (8, 128), 0)
    spots = jnp.full((8, 128), -1, jnp.int32)
    for s in range(MOST):
        least = jnp.min(jnp.min(left, axis=0, keepdims=True), axis=1, keepdims=True)
        left = jnp.where(left == least, float(rows), left)
        spots = jnp.where(row == s, least.astype(jnp.int32), spots)

    targets_ref[:128, :] = wanted
    targets_ref[128:, :] = spots


def pick_kernel(targets_ref, table, kept_ref, given_ref, found_ref):
    rows, width = table.shape
    targets = targets_ref[...]
    step = 512
    lanes = lax.broadcasted_iota(jnp.int32, (136, 128), 1)
    total = jnp.zeros((136, width), jnp.float32)
    for k in range(rows // step):
        hits = [targets == lanes + (k * step + l) for l in range(0, step, 128)]
        pick = jnp.concatenate([jnp.where(h, 1.0, 0.0).astype(jnp.bfloat16) for h in hits], axis=1)
        total = total + jnp.dot(pick, table[pl.ds(k * step, step), :], preferred_element_type=jnp.float32)
    kept_ref[...] = total[:64].astype(jnp.bfloat16)
    given_ref[...] = total[64:128].astype(jnp.bfloat16)
    found_ref[...] = total[128 : 128 + MOST].astype(jnp.bfloat16)


def settle_kernel(got_ref, block_ref):
    total = got_ref[0, :32, :].astype(jnp.float32)
    for z in range(1, 8):
        total = total + got_ref[z, :32, :].astype(jnp.float32)
    block_ref[:32, :] = total.astype(jnp.bfloat16)
    found = [got_ref[z, 32:, :].astype(jnp.float32) for z in range(8)]
    block_ref[32:, :] = jnp.concatenate(found, axis=0).astype(jnp.bfloat16)


def settled(got):
    vmem = pl.BlockSpec(memory_space=pltpu.VMEM)
    return pl.pallas_call(
        settle_kernel,
        out_shape=jax.ShapeDtypeStruct((64, got.shape[2]), jnp.bfloat16),
        in_specs=[vmem],
        out_specs=vmem,
        compiler_params=pltpu.CompilerParams(vmem_limit_bytes=8 << 20),
        cost_estimate=pl.CostEstimate(flops=1 << 20, bytes_accessed=1 << 20, transcendentals=0),
    )(got)


def own_picks(chosen_index, candidate_index, embeddings):
    rows, width = embeddings.shape
    index = jnp.concatenate([chosen_index, candidate_index]).reshape(5, 128)
    vmem = pl.BlockSpec(memory_space=pltpu.VMEM)
    targets = pl.pallas_call(
        functools.partial(spot_kernel, rows),
        out_shape=jax.ShapeDtypeStruct((136, 128), jnp.int32),
        in_specs=[vmem],
        out_specs=vmem,
        compiler_params=pltpu.CompilerParams(vmem_limit_bytes=8 << 20),
        cost_estimate=pl.CostEstimate(flops=1 << 32, bytes_accessed=1 << 17, transcendentals=0),
    )(index)
    return pl.pallas_call(
        pick_kernel,
        out_shape=[jax.ShapeDtypeStruct((64, width), jnp.bfloat16)] * 2
        + [jax.ShapeDtypeStruct((MOST, width), jnp.bfloat16)],
        in_specs=[vmem] * 2,
        out_specs=[vmem] * 3,
        compiler_params=pltpu.CompilerParams(vmem_limit_bytes=40 << 20),
        cost_estimate=pl.CostEstimate(flops=136 * 2048 * 768 * 2, bytes_accessed=4 << 20, transcendentals=0),
    )(targets, embeddings)


def local(embeddings, coverage, chosen_index, candidate_index):
    rows, width = embeddings.shape
    kept, given, found = own_picks(chosen_index, candidate_index, embeddings)
    half = kept + swap(given, 0, 1)
    quarter = half[:32] + swap(half[32:], 2, 0)
    send = jnp.concatenate([quarter, found], axis=0)
    send, later = lax.optimization_barrier((send, embeddings))
    partner = swap(later, 0, 1)
    got = lax.all_to_all(jnp.broadcast_to(send, (8, 32 + MOST, width)), "z", 0, 0)
    block = settled(got)
    line = jnp.stack([block] + [turn(block, s, True) for s in (1, 2, 3)])
    cands, chosen = line[:, :32].reshape(128, width), line[:, 32:].reshape(128, width)
    chosen = [chosen] + [turn(chosen, s, False) for s in (1, 2, 3)]
    cands = [cands] + [turn(cands, s, False) for s in (1, 2, 3)]

    table = [pltpu.VMEM((width, 256), jnp.bfloat16)]
    best = coverage.reshape(1, rows)
    for pieces in (chosen[:2], chosen[2:]):
        best = on_chip(best_kernel, [(2, rows)], table, 2, embeddings, best, *pieces, partner)[0]
    other = swap(best, 0, 1)
    turned = turned_pieces(cands)
    part, cover = on_chip(gain_kernel, [(128, 32), (1, rows)], [], 4, embeddings, best, other, turned, partner)
    parts = lax.all_to_all(part, CHIPS, 0, 0, tiled=True)
    gains = jnp.sum(lax.dynamic_slice_in_dim(parts, lax.axis_index("z") * 4, 4, 1), axis=0)
    return cover[0], gains


def solution(mesh):
    torus = Mesh(mesh.devices.reshape(SIZES), AXES)
    return jax.shard_map(
        local,
        mesh=torus,
        in_specs=(P(AXES, None), P(AXES), P(), P(BLK)),
        out_specs=(P(AXES), P(AXES)),
        check_vma=False,
    )
```
